768 devices in a mesh: bx: 48 (over z_lo, x, core), by: 16 (over z_hi, y).
Axes of the slice: x: 4, y: 8, z: 12 (z_hi: 2, z_lo: 6; z = z_hi * 6 + z_lo), core: 2. Of those that a mesh axis runs over, the one named last changes fastest.
Arguments:
- populations: float32 [19, 1, 6144, 2048], P(None, None, 'bx', 'by'), may hold values from 0 to 1, as said below
- solid_mask: int32 [1, 6144, 2048], P(None, 'bx', 'by'), may hold values 0 or 1
- pore_list: int32 [48, 16, 4], P('bx', 'by'), may hold values from 0 to 3, each once within a row
- pore_count: int32 [48, 16], P(None, 'by'), may hold values from 0 to 4, as said below
Outputs:
- final_populations: float32 [19, 1, 6144, 2048], P(None, None, 'bx', 'by')
The draws below stay inside these ranges and needn't reach their ends.
Inputs may be any that keep to these rules, and one draw needn't show every extreme that they name: Positive; each cell's populations are a perturbed equilibrium with velocity components of order 0.1. pore_count[i, j] + pore_count[(i + 24) mod 48, j] <= 4 for every i and j; some device has 4 pore blocks in every draw.
All inputs are finite; a program needn't handle non-finite values. No bound on the sum of `solid_mask` on one device may be relied on, other than what follows from the above.
Results may differ from the reference program's by a relative error of at most 0.0001.
Values sent between devices are 32-bit elements; how exact they have to be, the bound alone decides.
No kernel may reach another device: no remote copies, remote signals or barrier semaphores. Data moves between devices by JAX's collectives and lax.ppermute only.
A program may use at most 32 MiB of HBM per device.

```python
import jax
import jax.numpy as jnp
import numpy as np

BLOCK_SIDE = 64
BLOCK_SLOTS = 4
PLANES = 1
TIME_STEPS = 1
NX = 6144
NY = 2048
N_BX = 48
N_BY = 16


def draw_populations(key, part):
    key = jax.random.fold_in(key, 5)
    density_key, xkey_draw, ykey_draw, zkey_draw, jitter_key = jax.random.split(key, 5)
    grid_shape = (PLANES, NX, NY)
    density = jax.random.uniform(density_key, grid_shape, jnp.float32, 0.7, 1.3)
    spread = 0.1
    speed_x = jax.random.uniform(xkey_draw, grid_shape, jnp.float32, -spread, spread)
    speed_y = jax.random.uniform(ykey_draw, grid_shape, jnp.float32, -spread, spread)
    speed_z = jax.random.uniform(zkey_draw, grid_shape, jnp.float32, -spread, spread)
    velocity = jnp.array([[0, 0, 0], [1, 0, 0], [-1, 0, 0], [0, 1, 0], [0, -1, 0], [0, 0, 1], [0, 0, -1], [1, 1, 0], [-1, -1, 0], [1, -1, 0], [-1, 1, 0], [1, 0, 1], [-1, 0, -1], [1, 0, -1], [-1, 0, 1], [0, 1, 1], [0, -1, -1], [0, 1, -1], [0, -1, 1]], jnp.float32)
    weights = jnp.array([1.0 / 3.0] + [1.0 / 18.0] * 6 + [1.0 / 36.0] * 12, jnp.float32)
    dotted = velocity[:, 0, None, None, None] * speed_x + velocity[:, 1, None, None, None] * speed_y + velocity[:, 2, None, None, None] * speed_z
    square = speed_x * speed_x + speed_y * speed_y + speed_z * speed_z
    equilibrium = weights[:, None, None, None] * density * (1.0 + 3.0 * dotted + 4.5 * dotted * dotted - 1.5 * square)
    jitter = jax.random.uniform(jitter_key, (19,) + grid_shape, jnp.float32, 0.7, 1.3)
    return equilibrium * jitter


def draw_pore_count(key, part):
    key = jax.random.fold_in(key, 11)
    first_key, second_key, flip_key = jax.random.split(key, 3)
    halfway = N_BX // 2
    lower_counts = jax.random.randint(first_key, (halfway, N_BY), 0, BLOCK_SLOTS + 1)
    upper_counts = jax.random.randint(second_key, (halfway, N_BY), 0, BLOCK_SLOTS + 1 - lower_counts)
    flipped = jax.random.randint(flip_key, (halfway, N_BY), 0, 2)
    first_half = jnp.where(flipped == 1, upper_counts, lower_counts)
    second_half = jnp.where(flipped == 1, lower_counts, upper_counts)
    counts = jnp.concatenate([first_half, second_half], axis=0)
    counts = counts.at[0, 0].set(BLOCK_SLOTS).at[halfway, 0].set(0)
    return counts.astype(jnp.int32)


def with_ends(drawn, rng, smallest, largest):
    longest = drawn.shape.index(max(drawn.shape))
    spots = []
    for shift in (0, 1):
        where = [jax.random.randint(jax.random.fold_in(rng, axis), (), 0, length) for axis, length in enumerate(drawn.shape)]
        where[longest] = (where[longest] + shift) % drawn.shape[longest]
        spots.append(tuple(where))
    return drawn.at[spots[0]].set(smallest).at[spots[1]].set(largest)


def setup_inputs(seed: int = 0) -> dict:
    splits = jax.random.split(jax.random.key(seed), 5)
    return {
        "populations": draw_populations(jax.random.fold_in(splits[4], 71), 0),
        "solid_mask": with_ends((jax.random.randint(splits[1], (PLANES, NX, NY), 0, 5) < 2).astype(jnp.int32), jax.random.fold_in(splits[1], 1), 0, 1),
        "pore_list": jax.vmap(lambda own: jax.random.permutation(own, BLOCK_SLOTS))(jax.random.split(splits[2], N_BX * N_BY)).reshape((N_BX, N_BY, BLOCK_SLOTS)).astype(jnp.int32),
        "pore_count": draw_pore_count(jax.random.fold_in(splits[4], 71), 0),
    }


VELOCITY = np.array([[0, 0, 0], [1, 0, 0], [-1, 0, 0], [0, 1, 0], [0, -1, 0], [0, 0, 1], [0, 0, -1], [1, 1, 0], [-1, -1, 0], [1, -1, 0], [-1, 1, 0], [1, 0, 1], [-1, 0, -1], [1, 0, -1], [-1, 0, 1], [0, 1, 1], [0, -1, -1], [0, 1, -1], [0, -1, 1]])
WEIGHT = np.array([1.0 / 3.0] + [1.0 / 18.0] * 6 + [1.0 / 36.0] * 12)
OPPOSITE = np.array([0, 2, 1, 4, 3, 6, 5, 8, 7, 10, 9, 12, 11, 14, 13, 16, 15, 18, 17])
OMEGA_PLUS = 1.0 / 0.8
OMEGA_MINUS = 1.0 / (0.1875 / 0.3 + 0.5)


def collide(populations):
    extra_dims = (1,) * (populations.ndim - 1)
    along = [jnp.asarray(VELOCITY[:, a].reshape((19,) + extra_dims), populations.dtype) for a in range(3)]
    weights = jnp.asarray(WEIGHT.reshape((19,) + extra_dims), populations.dtype)
    density = jnp.sum(populations, axis=0)
    speed_x = jnp.sum(along[0] * populations, axis=0) / density
    speed_y = jnp.sum(along[1] * populations, axis=0) / density
    speed_z = jnp.sum(along[2] * populations, axis=0) / density
    dotted = along[0] * speed_x + along[1] * speed_y + along[2] * speed_z
    square = speed_x * speed_x + speed_y * speed_y + speed_z * speed_z
    equilibrium = weights * density * (1.0 + 3.0 * dotted + 4.5 * dotted * dotted - 1.5 * square)
    mirror = populations[OPPOSITE]
    emirror = equilibrium[OPPOSITE]
    even_part = 0.5 * (populations + mirror) - 0.5 * (equilibrium + emirror)
    odd_part = 0.5 * (populations - mirror) - 0.5 * (equilibrium - emirror)
    return populations - OMEGA_PLUS * even_part - OMEGA_MINUS * odd_part


def live_cells(pore_list, pore_count):
    positions = jnp.arange(BLOCK_SLOTS, dtype=jnp.int32)
    counted = positions[None, None, :] < pore_count[:, :, None]
    flags = jnp.stack([jnp.any(counted & (pore_list == b), axis=-1) for b in range(BLOCK_SLOTS)], axis=-1)
    flags = flags.reshape(N_BX, N_BY, 2, 2).transpose(0, 2, 1, 3).reshape(2 * N_BX, 2 * N_BY)
    return jnp.repeat(jnp.repeat(flags, BLOCK_SIDE, axis=0), BLOCK_SIDE, axis=1)


def stream(relaxed, populations, solid_mask, active):
    columns = []
    for k in range(19):
        step_x, step_y, step_z = (int(v) for v in VELOCITY[k])
        move = (step_z, step_x, step_y)
        shifted = jnp.roll(relaxed[k], move, axis=(0, 1, 2))
        blocked = jnp.roll(solid_mask, move, axis=(0, 1, 2)) != 0
        columns.append(jnp.where(blocked, relaxed[int(OPPOSITE[k])], shifted))
    passed = jnp.stack(columns)
    return jnp.where(active[None], passed, populations)


def reference(populations, solid_mask, pore_list, pore_count):
    live_columns = live_cells(pore_list, pore_count)[None, :, :]
    active = live_columns & (solid_mask == 0)
    for iteration in range(TIME_STEPS):
        relaxed = jnp.where(live_columns[None], collide(populations), populations)
        populations = stream(relaxed, populations, solid_mask, active)
    return populations
```

```python
import functools

import jax
import jax.numpy as jnp
from jax import lax
from jax.experimental import pallas as pl
from jax.experimental.pallas import tpu as pltpu
from jax.sharding import PartitionSpec as P

F32 = jnp.float32
SIDE = 128
TILES = SIDE // 8
CHUNKS = 4

PAIRS = (
    (1, 2, (1, 0, 0)),
    (3, 4, (0, 1, 0)),
    (5, 6, (0, 0, 1)),
    (7, 8, (1, 1, 0)),
    (9, 10, (1, -1, 0)),
    (11, 12, (1, 0, 1)),
    (13, 14, (1, 0, -1)),
    (15, 16, (0, 1, 1)),
    (17, 18, (0, 1, -1)),
)
VELOCITY = {0: (0, 0, 0)}
OPPOSITE = {0: 0}
for _k, _o, _c in PAIRS:
    VELOCITY[_k], VELOCITY[_o] = _c, tuple(-v for v in _c)
    OPPOSITE[_k], OPPOSITE[_o] = _o, _k
OMEGA_PLUS = 1.0 / 0.8
OMEGA_MINUS = 1.0 / (0.1875 / 0.3 + 0.5)

X_UP, X_DOWN = (1, 7, 9, 11, 13), (2, 8, 10, 12, 14)
Y_UP, Y_DOWN = (3, 7, 10, 15, 17), (4, 8, 9, 16, 18)
Y_ALL = Y_UP + Y_DOWN
REST = tuple(k for k in range(19) if k not in Y_ALL)
FLAG_ROW = (5, 6, 7, 5, 5)


def iota(axis):
    return lax.broadcasted_iota(jnp.int32, (8, SIDE), axis)


def relax(f):
    total = {p: f[k] + f[o] for p, (k, o, _) in enumerate(PAIRS)}
    diff = {p: f[k] - f[o] for p, (k, o, _) in enumerate(PAIRS)}
    density = ((total[0] + total[1]) + (total[2] + total[3])) + (
        (total[4] + total[5]) + (total[6] + total[7])
    )
    density = density + (total[8] + f[0])
    jx = (diff[0] + diff[3]) + (diff[4] + diff[5]) + diff[6]
    jy = (diff[1] + diff[3]) + (diff[7] - diff[4]) + diff[8]
    jz = (diff[2] + diff[5]) + (diff[7] - diff[6]) - diff[8]
    inverse = 1.0 / density
    speed = (jx * inverse, jy * inverse, jz * inverse)
    square = speed[0] * speed[0] + speed[1] * speed[1] + speed[2] * speed[2]
    base = 1.0 - 1.5 * square
    out = {0: f[0] - OMEGA_PLUS * (f[0] - (density * base) * (1.0 / 3.0))}
    for p, (k, o, c) in enumerate(PAIRS):
        weight = 1.0 / 18.0 if p < 3 else 1.0 / 36.0
        dotted = None
        for axis in range(3):
            if c[axis]:
                term = speed[axis] if c[axis] > 0 else -speed[axis]
                dotted = term if dotted is None else dotted + term
        scaled = density * weight
        even = 0.5 * total[p] - scaled * (base + 4.5 * (dotted * dotted))
        odd = 0.5 * diff[p] - scaled * (3.0 * dotted)
        out[k] = f[k] - OMEGA_PLUS * even - OMEGA_MINUS * odd
        out[o] = f[o] - OMEGA_PLUS * even + OMEGA_MINUS * odd
    return out


def collide_kernel(
    count_hbm, list_hbm, f_hbm, m_hbm,
    f_v, r_v, solid_v, active_v, chip_msg, off_msg, y_pre,
    count_ref, list_ref, mask_v, columns, sems,
):
    rows = SIDE // CHUNKS
    first = [
        pltpu.make_async_copy(source, target, sems.at[CHUNKS + n])
        for n, (source, target) in enumerate(
            ((count_hbm, count_ref), (list_hbm, list_ref), (m_hbm, mask_v))
        )
    ]
    copies = []
    for c in range(CHUNKS):
        part = pl.ds(c * rows, rows)
        copies.append(
            pltpu.make_async_copy(f_hbm.at[:, part, :], f_v.at[:, part, :], sems.at[c])
        )
    for copy in first + copies:
        copy.start()
    for copy in first:
        copy.wait()
    position = lax.axis_index("bx")
    count = count_ref[0, position]
    live = []
    for b in range(4):
        hit = jnp.int32(0)
        for s in range(4):
            found = jnp.logical_and(s < count, list_ref[0, 0, s] == b)
            hit = jnp.where(found, jnp.int32(1), hit)
        live.append(hit)
    lane, row = iota(1), iota(0)

    def tile(t, carry):
        at = pl.ds(pl.multiple_of(t * 8, 8), 8)
        low_half = t < TILES // 2
        left = jnp.where(low_half, live[0], live[2])
        right = jnp.where(low_half, live[1], live[3])
        is_live = jnp.where(lane < SIDE // 2, left, right) != 0
        f = [f_v[k, at, :] for k in range(19)]
        out = relax(f)
        out = [jnp.where(is_live, out[k], f[k]) for k in range(19)]
        for k in range(19):
            r_v[k, at, :] = out[k]
        solid = mask_v[at, :].astype(F32)
        solid_v[at, :] = solid
        active_v[at, :] = jnp.where(jnp.logical_and(is_live, solid == 0.0), 1.0, 0.0)
        packed = jnp.zeros((8, SIDE), F32)
        for start, edge, pops in ((0, SIDE - 1, Y_UP), (8, 0, Y_DOWN)):
            for n, k in enumerate(pops):
                packed = jnp.where(lane == start + n, out[k][:, edge : edge + 1], packed)
            flags = jnp.logical_and(lane >= start + 5, lane < start + 8)
            packed = jnp.where(flags, solid[:, edge : edge + 1], packed)
        columns[at, :] = packed
        return carry

    for c in range(CHUNKS):
        copies[c].wait()
        lax.fori_loop(c * (rows // 8), (c + 1) * (rows // 8), tile, 0)

    up = [r_v[k, SIDE - 1 : SIDE, :] for k in X_UP] + [solid_v[SIDE - 1 : SIDE, :]] * 3
    down = [r_v[k, 0:1, :] for k in X_DOWN] + [solid_v[0:1, :]] * 3
    up, down = jnp.concatenate(up, axis=0), jnp.concatenate(down, axis=0)
    even = lax.rem(position, 2) == 0
    chip_msg[...] = jnp.where(even, up, down)
    off_msg[...] = jnp.where(even, down, up)

    turned = jnp.transpose(columns[...])
    high, low = turned[0:8, :], turned[8:16, :]
    fore = jnp.logical_or(row == 1, row == 6)
    back = jnp.logical_or(row == 2, row == 7)
    y_pre[0] = jnp.where(
        fore, pltpu.roll(high, 1, 1), jnp.where(back, pltpu.roll(high, SIDE - 1, 1), high)
    )
    y_pre[1] = jnp.where(
        fore, pltpu.roll(low, SIDE - 1, 1), jnp.where(back, pltpu.roll(low, 1, 1), low)
    )
    for slab, flags, first, second in ((2, low, 0, 2), (3, high, 1, 3)):
        is_live = jnp.where(lane < SIDE // 2, live[first], live[second]) != 0
        free = jnp.broadcast_to(flags[5:6, :], (8, SIDE)) == 0.0
        y_pre[slab] = jnp.where(jnp.logical_and(is_live, free), 1.0, 0.0)


def halos(chip_ref, off_ref):
    parity = lax.rem(lax.axis_index("bx"), 2)
    chip, off = chip_ref[1 - parity], off_ref[...]
    return jnp.where(parity == 0, off, chip), jnp.where(parity == 0, chip, off)


def corner_kernel(y_pre, chip_ref, off_ref, near_msg, far_msg):
    low, high = halos(chip_ref, off_ref)
    lane, row = iota(1), iota(0)
    fore = jnp.logical_or(row == 1, row == 6)
    back = jnp.logical_or(row == 2, row == 7)
    first, last = lane == 0, lane == SIDE - 1
    up = jnp.where(jnp.logical_and(fore, first), pltpu.roll(low, 1, 1), y_pre[0])
    up = jnp.where(jnp.logical_and(back, last), high, up)
    down = jnp.where(jnp.logical_and(fore, last), pltpu.roll(high, SIDE - 1, 1), y_pre[1])
    down = jnp.where(jnp.logical_and(back, first), low, down)
    even = lax.rem(lax.axis_index("by"), 2) == 0
    near_msg[...] = jnp.where(even, up, down)
    far_msg[...] = jnp.where(even, down, up)


def stream_kernel(
    f_v, r_v, solid_v, active_v, chip_ref, off_ref, out_hbm, partial, stage, edges, sems
):
    low, high = halos(chip_ref, off_ref)
    edges[0], edges[1] = low, high
    lane, row = iota(1), iota(0)
    top, bottom = row == 0, row == 7
    first, last = lane == 0, lane == SIDE - 1

    def tile(t, carry):
        at = pl.ds(pl.multiple_of(t * 8, 8), 8)
        before = pl.ds(jnp.maximum(t * 8 - 1, 0), 1)
        after = pl.ds(jnp.minimum(t * 8 + 8, SIDE - 1), 1)

        def shift_x(block, row_before, row_after, step, halo_row):
            if step == 0:
                return block
            if step > 0:
                edge = jnp.where(t == 0, edges[0, halo_row : halo_row + 1, :], row_before())
                return jnp.where(top, edge, pltpu.roll(block, 1, 0))
            edge = jnp.where(t == TILES - 1, edges[1, halo_row : halo_row + 1, :], row_after())
            return jnp.where(bottom, edge, pltpu.roll(block, 7, 0))

        def shift_y(block, step):
            if step == 0:
                return block
            return pltpu.roll(block, 1 if step > 0 else SIDE - 1, 1)

        solid = solid_v[at, :]
        active = active_v[at, :] != 0.0
        blocked = {}
        for sx in (-1, 0, 1):
            moved = shift_x(
                solid, lambda: solid_v[before, :], lambda: solid_v[after, :], sx, 5
            )
            for sy in (-1, 0, 1):
                if sx or sy:
                    hit = shift_y(moved, sy) != 0.0
                    if sy:
                        hit = jnp.logical_or(hit, first if sy > 0 else last)
                    blocked[sx, sy] = hit
        own = [r_v[k, at, :] for k in range(19)]
        for k in range(19):
            sx, sy, _ = VELOCITY[k]
            moved = own[k]
            if sx:
                halo_row = X_UP.index(k) if sx > 0 else X_DOWN.index(k)
                moved = shift_x(
                    moved, lambda: r_v[k, before, :], lambda: r_v[k, after, :], sx, halo_row
                )
            moved = shift_y(moved, sy)
            if sx or sy:
                moved = jnp.where(blocked[sx, sy], own[OPPOSITE[k]], moved)
            result = jnp.where(active, moved, f_v[k, at, :])
            if k in Y_ALL:
                partial[Y_ALL.index(k), at, :] = result
            else:
                stage[REST.index(k), at, :] = result
        return carry

    lax.fori_loop(0, TILES, tile, 0)
    copies = [
        pltpu.make_async_copy(stage.at[n], out_hbm.at[k], sems.at[n]) for n, k in enumerate(REST)
    ]
    for copy in copies:
        copy.start()
    for copy in copies:
        copy.wait()


def patch_kernel(near_ref, far_ref, y_pre, partial, started, out_hbm, stage, sems):
    del started
    even = lax.rem(lax.axis_index("by"), 2) == 0
    near, far = near_ref[...], far_ref[...]
    below, above = jnp.where(even, far, near), jnp.where(even, near, far)
    flags = iota(0) >= 5
    free = [
        jnp.where(flags, jnp.where(message == 0.0, y_pre[slab], 0.0), message)
        for message, slab in ((below, 2), (above, 3))
    ]
    turned = jnp.transpose(
        jnp.concatenate(free + [jnp.zeros((SIDE - 16, SIDE), F32)], axis=0)
    )
    lane = lax.broadcasted_iota(jnp.int32, (SIDE, SIDE), 1)
    copies = []
    for n, k in enumerate(Y_ALL):
        side, which = n // 5, n % 5
        value = turned[:, side * 8 + which : side * 8 + which + 1]
        flag = side * 8 + FLAG_ROW[which]
        take = jnp.logical_and(
            lane == (0 if side == 0 else SIDE - 1), turned[:, flag : flag + 1] != 0.0
        )
        stage[n] = jnp.where(take, value, partial[n])
        copies.append(pltpu.make_async_copy(stage.at[n], out_hbm.at[k], sems.at[n]))
        copies[-1].start()
    for copy in copies:
        copy.wait()


def shape(*dims):
    return jax.ShapeDtypeStruct(dims, F32)


def in_vmem(*dims):
    return pltpu.VMEM(dims, F32)


def keep(x):
    return pltpu.with_memory_space_constraint(x, pltpu.VMEM)


def stay(x):
    return pltpu.with_memory_space_constraint(x, pltpu.HBM)


def pairs_of(count, first):
    pairs = []
    for low in range(first, count, 2):
        high = (low + 1) % count
        pairs += [(low, high), (high, low)]
    return sorted(pairs)


def local(n_bx, n_by, populations, solid_mask, pore_list, pore_count):
    vmem = pl.BlockSpec(memory_space=pltpu.VMEM)
    anywhere = pl.BlockSpec(memory_space=pl.ANY)
    plane = (SIDE, SIDE)
    f = populations.reshape(19, *plane)
    f_v, r_v, solid_v, active_v, chip_msg, off_msg, y_pre = pl.pallas_call(
        collide_kernel,
        out_shape=(
            in_vmem(19, *plane), in_vmem(19, *plane), in_vmem(*plane), in_vmem(*plane),
            in_vmem(8, SIDE), in_vmem(8, SIDE), in_vmem(4, 8, SIDE),
        ),
        in_specs=[pl.BlockSpec(memory_space=pltpu.HBM)] * 4,
        out_specs=[vmem] * 7,
        scratch_shapes=[
            pltpu.SMEM((1, n_bx), jnp.int32), pltpu.SMEM((1, 1, 4), jnp.int32),
            pltpu.VMEM(plane, jnp.int32), pltpu.VMEM(plane, F32),
            pltpu.SemaphoreType.DMA((CHUNKS + 3,)),
        ],
        compiler_params=pltpu.CompilerParams(vmem_limit_bytes=24 * 2**20),
        name="collide",
    )(stay(pore_count.T), stay(pore_list), stay(f), stay(solid_mask.reshape(plane)))

    off = lax.ppermute(off_msg, "bx", pairs_of(n_bx, 1))
    groups = [[low, low + 1] for low in range(0, n_bx, 2)]
    chip = lax.all_gather(chip_msg, "bx", axis_index_groups=groups)

    near_msg, far_msg = pl.pallas_call(
        corner_kernel,
        out_shape=(in_vmem(8, SIDE), in_vmem(8, SIDE)),
        in_specs=[vmem] * 3,
        out_specs=[vmem] * 2,
        name="corner",
    )(keep(y_pre), keep(chip), keep(off))

    near = lax.ppermute(near_msg, "by", pairs_of(n_by, 0))
    far = lax.ppermute(far_msg, "by", pairs_of(n_by, 1))

    out, partial = pl.pallas_call(
        stream_kernel,
        out_shape=(shape(19, *plane), in_vmem(10, *plane)),
        in_specs=[vmem] * 6,
        out_specs=[anywhere, vmem],
        scratch_shapes=[
            pltpu.VMEM((9, *plane), F32), pltpu.VMEM((2, 8, SIDE), F32),
            pltpu.SemaphoreType.DMA((9,)),
        ],
        compiler_params=pltpu.CompilerParams(vmem_limit_bytes=24 * 2**20),
        cost_estimate=pl.CostEstimate(
            flops=8_000_000, bytes_accessed=4_000_000, transcendentals=0
        ),
        name="stream",
    )(keep(f_v), keep(r_v), keep(solid_v), keep(active_v), keep(chip), keep(off))

    out = pl.pallas_call(
        patch_kernel,
        out_shape=shape(19, *plane),
        in_specs=[vmem] * 4 + [anywhere],
        out_specs=anywhere,
        scratch_shapes=[pltpu.VMEM((10, *plane), F32), pltpu.SemaphoreType.DMA((10,))],
        input_output_aliases={4: 0},
        compiler_params=pltpu.CompilerParams(vmem_limit_bytes=24 * 2**20),
        name="patch",
    )(keep(near), keep(far), keep(y_pre), keep(partial), out)
    return out.reshape(19, 1, *plane)


def solution(mesh):
    placed = (P(None, None, "bx", "by"), P(None, "bx", "by"), P("bx", "by", None), P(None, "by"))
    return jax.shard_map(
        functools.partial(local, mesh.shape["bx"], mesh.shape["by"]),
        mesh=mesh,
        in_specs=placed,
        out_specs=P(None, None, "bx", "by"),
        check_vma=False,
    )
```

```python
import functools

import jax
import jax.numpy as jnp
from jax import lax
from jax.experimental import pallas as pl
from jax.experimental.pallas import tpu as pltpu
from jax.sharding import PartitionSpec as P

F32 = jnp.float32
SIDE = 128
TILES = SIDE // 8
CHUNKS = 4

PAIRS = (
    (1, 2, (1, 0, 0)),
    (3, 4, (0, 1, 0)),
    (5, 6, (0, 0, 1)),
    (7, 8, (1, 1, 0)),
    (9, 10, (1, -1, 0)),
    (11, 12, (1, 0, 1)),
    (13, 14, (1, 0, -1)),
    (15, 16, (0, 1, 1)),
    (17, 18, (0, 1, -1)),
)
VELOCITY = {0: (0, 0, 0)}
OPPOSITE = {0: 0}
for _k, _o, _c in PAIRS:
    VELOCITY[_k], VELOCITY[_o] = _c, tuple(-v for v in _c)
    OPPOSITE[_k], OPPOSITE[_o] = _o, _k
OMEGA_PLUS = 1.0 / 0.8
OMEGA_MINUS = 1.0 / (0.1875 / 0.3 + 0.5)

X_UP, X_DOWN = (1, 7, 9, 11, 13), (2, 8, 10, 12, 14)
Y_UP, Y_DOWN = (3, 7, 10, 15, 17), (4, 8, 9, 16, 18)
Y_ALL = Y_UP + Y_DOWN
X_ALL = X_UP + X_DOWN
REST = tuple(k for k in range(19) if k not in Y_ALL)
FLAG_ROW = (5, 6, 7, 5, 5)


def iota(axis):
    return lax.broadcasted_iota(jnp.int32, (8, SIDE), axis)


def relax(f):
    total = {p: f[k] + f[o] for p, (k, o, _) in enumerate(PAIRS)}
    diff = {p: f[k] - f[o] for p, (k, o, _) in enumerate(PAIRS)}
    density = ((total[0] + total[1]) + (total[2] + total[3])) + (
        (total[4] + total[5]) + (total[6] + total[7])
    )
    density = density + (total[8] + f[0])
    jx = (diff[0] + diff[3]) + (diff[4] + diff[5]) + diff[6]
    jy = (diff[1] + diff[3]) + (diff[7] - diff[4]) + diff[8]
    jz = (diff[2] + diff[5]) + (diff[7] - diff[6]) - diff[8]
    inverse = 1.0 / density
    speed = (jx * inverse, jy * inverse, jz * inverse)
    square = speed[0] * speed[0] + speed[1] * speed[1] + speed[2] * speed[2]
    base = 1.0 - 1.5 * square
    out = {0: f[0] - OMEGA_PLUS * (f[0] - (density * base) * (1.0 / 3.0))}
    for p, (k, o, c) in enumerate(PAIRS):
        weight = 1.0 / 18.0 if p < 3 else 1.0 / 36.0
        dotted = None
        for axis in range(3):
            if c[axis]:
                term = speed[axis] if c[axis] > 0 else -speed[axis]
                dotted = term if dotted is None else dotted + term
        scaled = density * weight
        even = 0.5 * total[p] - scaled * (base + 4.5 * (dotted * dotted))
        odd = 0.5 * diff[p] - scaled * (3.0 * dotted)
        out[k] = f[k] - OMEGA_PLUS * even - OMEGA_MINUS * odd
        out[o] = f[o] - OMEGA_PLUS * even + OMEGA_MINUS * odd
    return out


def is_early():
    return jnp.logical_and(
        lax.axis_index("bx") < lax.axis_size("bx") // 2,
        lax.axis_index("by") < lax.axis_size("by") // 2,
    )


def stream_interior(f_v, r_v, solid_v, active_v, partial):
    lane, row = iota(1), iota(0)
    first, last = lane == 0, lane == SIDE - 1

    def tile(t, carry):
        at = pl.ds(pl.multiple_of(t * 8, 8), 8)
        before = pl.ds(jnp.maximum(t * 8 - 1, 0), 1)
        after = pl.ds(jnp.minimum(t * 8 + 8, SIDE - 1), 1)
        top, bottom = row == 0, row == 7
        outer_top = row == jnp.where(t == 0, 0, -1)
        outer_bottom = row == jnp.where(t == TILES - 1, 7, -1)

        def shift_x(ref, block, step):
            if step > 0:
                return jnp.where(top, ref[before, :], pltpu.roll(block, 1, 0))
            if step < 0:
                return jnp.where(bottom, ref[after, :], pltpu.roll(block, 7, 0))
            return block

        def shift_y(block, step):
            return pltpu.roll(block, 1 if step > 0 else SIDE - 1, 1) if step else block

        solid = solid_v[at, :]
        active = active_v[at, :] != 0.0
        blocked = {}
        for sx in (-1, 0, 1):
            moved = shift_x(solid_v, solid, sx)
            for sy in (-1, 0, 1):
                if sx or sy:
                    hit = shift_y(moved, sy) != 0.0
                    if sx:
                        hit = jnp.logical_or(hit, outer_top if sx > 0 else outer_bottom)
                    if sy:
                        hit = jnp.logical_or(hit, first if sy > 0 else last)
                    blocked[sx, sy] = hit
        own = [r_v[k, at, :] for k in range(19)]
        for k in range(19):
            sx, sy, _ = VELOCITY[k]
            moved = shift_y(shift_x(r_v.at[k], own[k], sx), sy)
            if sx or sy:
                moved = jnp.where(blocked[sx, sy], own[OPPOSITE[k]], moved)
            partial[k, at, :] = jnp.where(active, moved, f_v[k, at, :])
        return carry

    lax.fori_loop(0, TILES, tile, 0)


def collide_kernel(
    count_hbm, list_hbm, f_hbm, m_hbm,
    f_v, r_v, solid_v, active_v, near_msg, far_msg, y_active, partial,
    count_ref, list_ref, mask_v, columns, sems,
):
    rows = SIDE // CHUNKS
    first = [
        pltpu.make_async_copy(source, target, sems.at[CHUNKS + n])
        for n, (source, target) in enumerate(
            ((count_hbm, count_ref), (list_hbm, list_ref), (m_hbm, mask_v))
        )
    ]
    copies = []
    for c in range(CHUNKS):
        part = pl.ds(c * rows, rows)
        copies.append(
            pltpu.make_async_copy(f_hbm.at[:, part, :], f_v.at[:, part, :], sems.at[c])
        )
    for copy in first + copies:
        copy.start()
    for copy in first:
        copy.wait()
    position = lax.axis_index("bx")
    count = count_ref[0, position]
    live = []
    for b in range(4):
        hit = jnp.int32(0)
        for s in range(4):
            found = jnp.logical_and(s < count, list_ref[0, 0, s] == b)
            hit = jnp.where(found, jnp.int32(1), hit)
        live.append(hit)
    lane = iota(1)

    def tile(t, carry):
        at = pl.ds(pl.multiple_of(t * 8, 8), 8)
        low_half = t < TILES // 2
        left = jnp.where(low_half, live[0], live[2])
        right = jnp.where(low_half, live[1], live[3])
        is_live = jnp.where(lane < SIDE // 2, left, right) != 0
        f = [f_v[k, at, :] for k in range(19)]
        out = relax(f)
        out = [jnp.where(is_live, out[k], f[k]) for k in range(19)]
        for k in range(19):
            r_v[k, at, :] = out[k]
        solid = mask_v[at, :].astype(F32)
        solid_v[at, :] = solid
        active_v[at, :] = jnp.where(jnp.logical_and(is_live, solid == 0.0), 1.0, 0.0)
        packed = jnp.zeros((8, SIDE), F32)
        for start, edge, pops in ((0, SIDE - 1, Y_UP), (8, 0, Y_DOWN)):
            for n, k in enumerate(pops):
                packed = jnp.where(lane == start + n, out[k][:, edge : edge + 1], packed)
            flags = jnp.logical_and(lane >= start + 5, lane < start + 8)
            packed = jnp.where(flags, solid[:, edge : edge + 1], packed)
        columns[at, :] = packed
        return carry

    for c in range(CHUNKS):
        copies[c].wait()
        lax.fori_loop(c * (rows // 8), (c + 1) * (rows // 8), tile, 0)

    turned = jnp.transpose(columns[...])
    up, down = turned[0:8, :], turned[8:16, :]
    even = lax.rem(lax.axis_index("by"), 2) == 0
    near_msg[...] = jnp.where(even, up, down)
    far_msg[...] = jnp.where(even, down, up)
    for slab, flags in ((0, down), (1, up)):
        is_live = jnp.where(lane < SIDE // 2, live[slab], live[2 + slab]) != 0
        free = jnp.broadcast_to(flags[5:6, :], (8, SIDE)) == 0.0
        y_active[slab] = jnp.where(jnp.logical_and(is_live, free), 1.0, 0.0)

    @pl.when(is_early())
    def _():
        stream_interior(f_v, r_v, solid_v, active_v, partial)


def stream_kernel(f_v, r_v, solid_v, active_v, begun, partial):
    del begun

    @pl.when(jnp.logical_not(is_early()))
    def _():
        stream_interior(f_v, r_v, solid_v, active_v, partial)


def from_sides(axis, near_ref, far_ref):
    even = lax.rem(lax.axis_index(axis), 2) == 0
    near, far = near_ref[...], far_ref[...]
    return jnp.where(even, far, near), jnp.where(even, near, far)


def corner_kernel(r_v, solid_v, partial, far_ref, near_ref, chip_msg, off_msg, wrap_msg):
    del partial
    below, above = from_sides("by", near_ref, far_ref)
    lane, row = iota(1), iota(0)
    fore = jnp.logical_or(row == 1, row == 6)
    back = jnp.logical_or(row == 2, row == 7)

    def message(pops, x, from_below, from_above):
        edge = pl.ds(x, 1)
        rows = [r_v[k, edge, :] for k in pops] + [solid_v[edge, :]] * 3
        rows = jnp.concatenate(rows, axis=0)
        lower = jnp.broadcast_to(below[:, x : x + 1], (8, SIDE))
        upper = jnp.broadcast_to(above[:, x : x + 1], (8, SIDE))
        raised = jnp.where(lane == 0, lower, pltpu.roll(rows, 1, 1))
        lowered = jnp.where(lane == SIDE - 1, upper, pltpu.roll(rows, SIDE - 1, 1))
        return jnp.where(from_below, raised, jnp.where(from_above, lowered, rows))

    up = message(X_UP, SIDE - 1, fore, back)
    down = message(X_DOWN, 0, back, fore)
    even = lax.rem(lax.axis_index("bx"), 2) == 0
    chip_msg[...] = jnp.where(even, up, down)
    off_msg[...] = jnp.where(even, down, up)
    wrap_msg[...] = jnp.where(even, down, up)


def y_patch_kernel(far_ref, near_ref, y_active, partial, out_hbm, edges, stage, sems):
    copies = [
        pltpu.make_async_copy(partial.at[k], out_hbm.at[k], sems.at[10 + n])
        for n, k in enumerate(REST)
    ]
    for copy in copies:
        copy.start()
    below, above = from_sides("by", near_ref, far_ref)
    flags = iota(0) >= 5
    messages = []
    lane8, row8 = iota(1), iota(0)
    fore = jnp.logical_or(row8 == 1, row8 == 6)
    back = jnp.logical_or(row8 == 2, row8 == 7)
    for message, slab, step in ((below, 0, 1), (above, 1, -1)):
        raised, lowered = pltpu.roll(message, 1, 1), pltpu.roll(message, SIDE - 1, 1)
        ahead, behind = (fore, back) if step > 0 else (back, fore)
        moved = jnp.where(ahead, raised, jnp.where(behind, lowered, message))
        outside = jnp.logical_or(
            jnp.logical_and(ahead, lane8 == 0), jnp.logical_and(behind, lane8 == SIDE - 1)
        )
        free = jnp.logical_and(moved == 0.0, jnp.logical_not(outside))
        messages.append(jnp.where(flags, jnp.where(free, y_active[slab], 0.0), moved))
    turned = jnp.transpose(
        jnp.concatenate(messages + [jnp.zeros((SIDE - 16, SIDE), F32)], axis=0)
    )
    lane = lax.broadcasted_iota(jnp.int32, (SIDE, SIDE), 1)
    for n, k in enumerate(Y_ALL):
        side, which = n // 5, n % 5
        value = turned[:, side * 8 + which : side * 8 + which + 1]
        flag = side * 8 + FLAG_ROW[which]
        take = jnp.logical_and(
            lane == (0 if side == 0 else SIDE - 1), turned[:, flag : flag + 1] != 0.0
        )
        stage[n] = jnp.where(take, value, partial[k])
        copies.append(pltpu.make_async_copy(stage.at[n], out_hbm.at[k], sems.at[n]))
        copies[-1].start()
    for n, k in enumerate(X_ALL):
        at = pl.ds(0 if n < 5 else SIDE - 8, 8)
        edges[n] = stage[Y_ALL.index(k), at, :] if k in Y_ALL else partial[k, at, :]
    for copy in copies:
        copy.wait()


def x_patch_kernel(off_ref, chip_ref, wrap_ref, active_v, edges, started, out_hbm, stage, sems):
    del started
    position = lax.axis_index("bx")
    outer = jnp.logical_or(position == 0, position == lax.axis_size("bx") - 1)
    even = lax.rem(position, 2) == 0
    chip, off = chip_ref[...], jnp.where(outer, wrap_ref[...], off_ref[...])
    below, above = jnp.where(even, off, chip), jnp.where(even, chip, off)
    row = iota(0)
    copies = []
    for n, k in enumerate(X_ALL):
        side, which = n // 5, n % 5
        message = below if side == 0 else above
        at = pl.ds(0 if side == 0 else SIDE - 8, 8)
        flag = FLAG_ROW[which]
        take = jnp.logical_and(active_v[at, :] != 0.0, message[flag : flag + 1, :] == 0.0)
        take = jnp.logical_and(take, row == (0 if side == 0 else 7))
        stage[n] = jnp.where(take, message[which : which + 1, :], edges[n])
        copies.append(pltpu.make_async_copy(stage.at[n], out_hbm.at[k, at, :], sems.at[n]))
        copies[-1].start()
    for copy in copies:
        copy.wait()


def shape(*dims):
    return jax.ShapeDtypeStruct(dims, F32)


def in_vmem(*dims):
    return pltpu.VMEM(dims, F32)


def keep(x):
    return pltpu.with_memory_space_constraint(x, pltpu.VMEM)


def stay(x):
    return pltpu.with_memory_space_constraint(x, pltpu.HBM)


def pairs_of(first, last):
    pairs = []
    for low in range(first, last, 2):
        pairs += [(low, low + 1), (low + 1, low)]
    return pairs


def wrap_pairs(count):
    return [(count - 1, 0), (0, count - 1)]


def local(n_bx, n_by, populations, solid_mask, pore_list, pore_count):
    vmem = pl.BlockSpec(memory_space=pltpu.VMEM)
    anywhere = pl.BlockSpec(memory_space=pl.ANY)
    params = pltpu.CompilerParams(vmem_limit_bytes=24 * 2**20)
    plane = (SIDE, SIDE)
    f = populations.reshape(19, *plane)
    f_v, r_v, solid_v, active_v, near_msg, far_msg, y_active, partial = pl.pallas_call(
        collide_kernel,
        out_shape=(
            in_vmem(19, *plane), in_vmem(19, *plane), in_vmem(*plane), in_vmem(*plane),
            in_vmem(8, SIDE), in_vmem(8, SIDE), in_vmem(2, 8, SIDE), in_vmem(19, *plane),
        ),
        in_specs=[pl.BlockSpec(memory_space=pltpu.HBM)] * 4,
        out_specs=[vmem] * 8,
        scratch_shapes=[
            pltpu.SMEM((1, n_bx), jnp.int32), pltpu.SMEM((1, 1, 4), jnp.int32),
            pltpu.VMEM(plane, jnp.int32), pltpu.VMEM(plane, F32),
            pltpu.SemaphoreType.DMA((CHUNKS + 3,)),
        ],
        compiler_params=params,
        name="collide",
    )(stay(pore_count.T), stay(pore_list), stay(f), stay(solid_mask.reshape(plane)))

    far = lax.ppermute(far_msg, "by", pairs_of(1, n_by - 1) + wrap_pairs(n_by))
    near = lax.ppermute(near_msg, "by", pairs_of(0, n_by))

    partial = pl.pallas_call(
        stream_kernel,
        out_shape=in_vmem(19, *plane),
        in_specs=[vmem] * 5,
        out_specs=vmem,
        input_output_aliases={4: 0},
        compiler_params=params,
        cost_estimate=pl.CostEstimate(
            flops=8_000_000, bytes_accessed=4_000_000, transcendentals=0
        ),
        name="stream",
    )(keep(f_v), keep(r_v), keep(solid_v), keep(active_v), keep(partial))

    chip_msg, off_msg, wrap_msg = pl.pallas_call(
        corner_kernel,
        out_shape=(in_vmem(8, SIDE),) * 3,
        in_specs=[vmem] * 5,
        out_specs=[vmem] * 3,
        compiler_params=params,
        name="corner",
    )(keep(r_v), keep(solid_v), keep(partial), keep(far), keep(near))

    off = lax.ppermute(off_msg, "bx", pairs_of(1, n_bx - 1))
    chip = lax.ppermute(chip_msg, "bx", pairs_of(0, n_bx))
    wrap = lax.ppermute(wrap_msg, "bx", wrap_pairs(n_bx))

    out, edges = pl.pallas_call(
        y_patch_kernel,
        out_shape=(shape(19, *plane), in_vmem(10, 8, SIDE)),
        in_specs=[vmem] * 4,
        out_specs=[anywhere, vmem],
        scratch_shapes=[pltpu.VMEM((10, *plane), F32), pltpu.SemaphoreType.DMA((19,))],
        compiler_params=params,
        cost_estimate=pl.CostEstimate(
            flops=8_000_000, bytes_accessed=4_000_000, transcendentals=0
        ),
        name="y_patch",
    )(keep(far), keep(near), keep(y_active), keep(partial))

    out = pl.pallas_call(
        x_patch_kernel,
        out_shape=shape(19, *plane),
        in_specs=[vmem] * 5 + [anywhere],
        out_specs=anywhere,
        scratch_shapes=[pltpu.VMEM((10, 8, SIDE), F32), pltpu.SemaphoreType.DMA((10,))],
        input_output_aliases={5: 0},
        compiler_params=params,
        name="x_patch",
    )(keep(off), keep(chip), keep(wrap), keep(active_v), keep(edges), out)
    return out.reshape(19, 1, *plane)


def solution(mesh):
    placed = (P(None, None, "bx", "by"), P(None, "bx", "by"), P("bx", "by", None), P(None, "by"))
    return jax.shard_map(
        functools.partial(local, mesh.shape["bx"], mesh.shape["by"]),
        mesh=mesh,
        in_specs=placed,
        out_specs=P(None, None, "bx", "by"),
        check_vma=False,
    )
```

```python
import functools

import jax
import jax.numpy as jnp
from jax import lax
from jax.experimental import pallas as pl
from jax.experimental.pallas import tpu as pltpu
from jax.sharding import PartitionSpec as P

F32 = jnp.float32
SIDE = 128
TILES = SIDE // 8
CHUNKS = 4

PAIRS = (
    (1, 2, (1, 0, 0)),
    (3, 4, (0, 1, 0)),
    (5, 6, (0, 0, 1)),
    (7, 8, (1, 1, 0)),
    (9, 10, (1, -1, 0)),
    (11, 12, (1, 0, 1)),
    (13, 14, (1, 0, -1)),
    (15, 16, (0, 1, 1)),
    (17, 18, (0, 1, -1)),
)
VELOCITY = {0: (0, 0, 0)}
OPPOSITE = {0: 0}
for _k, _o, _c in PAIRS:
    VELOCITY[_k], VELOCITY[_o] = _c, tuple(-v for v in _c)
    OPPOSITE[_k], OPPOSITE[_o] = _o, _k
OMEGA_PLUS = 1.0 / 0.8
OMEGA_MINUS = 1.0 / (0.1875 / 0.3 + 0.5)

X_UP, X_DOWN = (1, 7, 9, 11, 13), (2, 8, 10, 12, 14)
Y_UP, Y_DOWN = (3, 7, 10, 15, 17), (4, 8, 9, 16, 18)
Y_ALL = Y_UP + Y_DOWN
REST = tuple(k for k in range(19) if k not in Y_ALL)
FLAG_ROW = (5, 6, 7, 5, 5)


def iota(axis):
    return lax.broadcasted_iota(jnp.int32, (8, SIDE), axis)


def relax(f):
    total = {p: f[k] + f[o] for p, (k, o, _) in enumerate(PAIRS)}
    diff = {p: f[k] - f[o] for p, (k, o, _) in enumerate(PAIRS)}
    density = ((total[0] + total[1]) + (total[2] + total[3])) + (
        (total[4] + total[5]) + (total[6] + total[7])
    )
    density = density + (total[8] + f[0])
    jx = (diff[0] + diff[3]) + (diff[4] + diff[5]) + diff[6]
    jy = (diff[1] + diff[3]) + (diff[7] - diff[4]) + diff[8]
    jz = (diff[2] + diff[5]) + (diff[7] - diff[6]) - diff[8]
    inverse = 1.0 / density
    speed = (jx * inverse, jy * inverse, jz * inverse)
    square = speed[0] * speed[0] + speed[1] * speed[1] + speed[2] * speed[2]
    base = 1.0 - 1.5 * square
    out = {0: f[0] - OMEGA_PLUS * (f[0] - (density * base) * (1.0 / 3.0))}
    for p, (k, o, c) in enumerate(PAIRS):
        weight = 1.0 / 18.0 if p < 3 else 1.0 / 36.0
        dotted = None
        for axis in range(3):
            if c[axis]:
                term = speed[axis] if c[axis] > 0 else -speed[axis]
                dotted = term if dotted is None else dotted + term
        scaled = density * weight
        even = 0.5 * total[p] - scaled * (base + 4.5 * (dotted * dotted))
        odd = 0.5 * diff[p] - scaled * (3.0 * dotted)
        out[k] = f[k] - OMEGA_PLUS * even - OMEGA_MINUS * odd
        out[o] = f[o] - OMEGA_PLUS * even + OMEGA_MINUS * odd
    return out


def is_early():
    position = lax.axis_index("bx") + lax.axis_index("by")
    return jnp.logical_and(
        jnp.logical_and(
            lax.axis_index("bx") < lax.axis_size("bx") // 2,
            lax.axis_index("by") < lax.axis_size("by") // 2,
        ),
        position > 0,
    )


def live_blocks(count_ref, list_ref):
    count = count_ref[0, lax.axis_index("bx")]
    live = []
    for b in range(4):
        hit = jnp.int32(0)
        for s in range(4):
            found = jnp.logical_and(s < count, list_ref[0, 0, s] == b)
            hit = jnp.where(found, jnp.int32(1), hit)
        live.append(hit)
    return live


def live_lanes(live, t):
    low_half = t < TILES // 2
    left = jnp.where(low_half, live[0], live[2])
    right = jnp.where(low_half, live[1], live[3])
    return jnp.where(iota(1) < SIDE // 2, left, right) != 0


def collide_block(count_ref, list_ref, f_v, mask_v, r_v, solid_v, active_v, y_pre, columns):
    live = live_blocks(count_ref, list_ref)
    lane, row = iota(1), iota(0)

    def tile(t, carry):
        at = pl.ds(pl.multiple_of(t * 8, 8), 8)
        is_live = live_lanes(live, t)
        f = [f_v[k, at, :] for k in range(19)]
        out = relax(f)
        out = [jnp.where(is_live, out[k], f[k]) for k in range(19)]
        for k in range(19):
            r_v[k, at, :] = out[k]
        solid = mask_v[at, :].astype(F32)
        solid_v[at, :] = solid
        active_v[at, :] = jnp.where(jnp.logical_and(is_live, solid == 0.0), 1.0, 0.0)
        packed = jnp.zeros((8, SIDE), F32)
        for start, edge, pops in ((0, SIDE - 1, Y_UP), (8, 0, Y_DOWN)):
            for n, k in enumerate(pops):
                packed = jnp.where(lane == start + n, out[k][:, edge : edge + 1], packed)
            flags = jnp.logical_and(lane >= start + 5, lane < start + 8)
            packed = jnp.where(flags, solid[:, edge : edge + 1], packed)
        columns[at, :] = packed
        return carry

    lax.fori_loop(0, TILES, tile, 0)

    turned = jnp.transpose(columns[...])
    high, low = turned[0:8, :], turned[8:16, :]
    fore = jnp.logical_or(row == 1, row == 6)
    back = jnp.logical_or(row == 2, row == 7)
    y_pre[0] = jnp.where(
        fore, pltpu.roll(high, 1, 1), jnp.where(back, pltpu.roll(high, SIDE - 1, 1), high)
    )
    y_pre[1] = jnp.where(
        fore, pltpu.roll(low, SIDE - 1, 1), jnp.where(back, pltpu.roll(low, 1, 1), low)
    )
    for slab, flags, first, second in ((2, low, 0, 2), (3, high, 1, 3)):
        is_live = jnp.where(lane < SIDE // 2, live[first], live[second]) != 0
        free = jnp.broadcast_to(flags[5:6, :], (8, SIDE)) == 0.0
        y_pre[slab] = jnp.where(jnp.logical_and(is_live, free), 1.0, 0.0)


def rim_kernel(
    count_hbm, list_hbm, f_hbm, m_hbm,
    chip_msg, off_msg, f_v, mask_v, r_v, solid_v, active_v, y_pre,
    edge_f, edge_m, count_ref, list_ref, columns, sems,
):
    ends = (pl.ds(SIDE - 8, 8), pl.ds(0, 8))
    pairs = [(count_hbm, count_ref), (list_hbm, list_ref)]
    for n, end in enumerate(ends):
        pairs += [(m_hbm.at[end, :], edge_m.at[n]), (f_hbm.at[:, end, :], edge_f.at[n])]
    first = len(pairs)
    pairs += [(m_hbm, mask_v)]
    for c in range(CHUNKS):
        part = pl.ds(c * (SIDE // CHUNKS), SIDE // CHUNKS)
        pairs.append((f_hbm.at[:, part, :], f_v.at[:, part, :]))
    copies = [pltpu.make_async_copy(s, t, sems.at[n]) for n, (s, t) in enumerate(pairs)]
    for copy in copies:
        copy.start()
    for copy in copies[:first]:
        copy.wait()
    live = live_blocks(count_ref, list_ref)
    messages = []
    for n, (pops, inner) in enumerate(((X_UP, 7), (X_DOWN, 0))):
        f = [edge_f[n, k] for k in range(19)]
        out = relax(f)
        is_live = live_lanes(live, TILES - 1 if n == 0 else 0)
        solid = edge_m[n].astype(F32)
        rows = [jnp.where(is_live, out[k], f[k])[inner : inner + 1, :] for k in pops]
        rows += [solid[inner : inner + 1, :]] * 3
        messages.append(jnp.concatenate(rows, axis=0))
    up, down = messages
    even = lax.rem(lax.axis_index("bx"), 2) == 0
    chip_msg[...] = jnp.where(even, up, down)
    off_msg[...] = jnp.where(even, down, up)
    for copy in copies[first:]:
        copy.wait()

    @pl.when(is_early())
    def _():
        collide_block(
            count_ref, list_ref, f_v, mask_v, r_v, solid_v, active_v, y_pre, columns
        )


def collide_kernel(
    count_ref, list_ref, f_v, mask_v, r_in, solid_in, active_in, y_in,
    r_v, solid_v, active_v, y_pre, columns,
):
    del r_in, solid_in, active_in, y_in

    @pl.when(jnp.logical_not(is_early()))
    def _():
        collide_block(
            count_ref, list_ref, f_v, mask_v, r_v, solid_v, active_v, y_pre, columns
        )


def halos(chip_ref, off_ref):
    parity = lax.rem(lax.axis_index("bx"), 2)
    chip, off = chip_ref[...], off_ref[...]
    return jnp.where(parity == 0, off, chip), jnp.where(parity == 0, chip, off)


def corner_kernel(y_pre, chip_ref, off_ref, first_msg, far_msg, second_msg):
    low, high = halos(chip_ref, off_ref)
    lane, row = iota(1), iota(0)
    fore = jnp.logical_or(row == 1, row == 6)
    back = jnp.logical_or(row == 2, row == 7)
    first, last = lane == 0, lane == SIDE - 1
    up = jnp.where(jnp.logical_and(fore, first), pltpu.roll(low, 1, 1), y_pre[0])
    up = jnp.where(jnp.logical_and(back, last), high, up)
    down = jnp.where(jnp.logical_and(fore, last), pltpu.roll(high, SIDE - 1, 1), y_pre[1])
    down = jnp.where(jnp.logical_and(back, first), low, down)
    even = lax.rem(lax.axis_index("by"), 2) == 0
    first_msg[...] = jnp.where(even, up, down)
    far_msg[...] = jnp.where(even, down, up)
    second_msg[...] = jnp.where(even, up, down)


def stream_kernel(
    f_v, r_v, solid_v, active_v, chip_ref, off_ref, out_hbm, partial, stage, edges, sems
):
    low, high = halos(chip_ref, off_ref)
    edges[0], edges[1] = low, high
    lane, row = iota(1), iota(0)
    top, bottom = row == 0, row == 7
    first, last = lane == 0, lane == SIDE - 1

    def tile(t, carry):
        at = pl.ds(pl.multiple_of(t * 8, 8), 8)
        before = pl.ds(jnp.maximum(t * 8 - 1, 0), 1)
        after = pl.ds(jnp.minimum(t * 8 + 8, SIDE - 1), 1)

        def shift_x(block, row_before, row_after, step, halo_row):
            if step == 0:
                return block
            if step > 0:
                edge = jnp.where(t == 0, edges[0, halo_row : halo_row + 1, :], row_before())
                return jnp.where(top, edge, pltpu.roll(block, 1, 0))
            edge = jnp.where(t == TILES - 1, edges[1, halo_row : halo_row + 1, :], row_after())
            return jnp.where(bottom, edge, pltpu.roll(block, 7, 0))

        def shift_y(block, step):
            if step == 0:
                return block
            return pltpu.roll(block, 1 if step > 0 else SIDE - 1, 1)

        solid = solid_v[at, :]
        active = active_v[at, :] != 0.0
        blocked = {}
        for sx in (-1, 0, 1):
            moved = shift_x(
                solid, lambda: solid_v[before, :], lambda: solid_v[after, :], sx, 5
            )
            for sy in (-1, 0, 1):
                if sx or sy:
                    hit = shift_y(moved, sy) != 0.0
                    if sy:
                        hit = jnp.logical_or(hit, first if sy > 0 else last)
                    blocked[sx, sy] = hit
        own = [r_v[k, at, :] for k in range(19)]
        for k in range(19):
            sx, sy, _ = VELOCITY[k]
            moved = own[k]
            if sx:
                halo_row = X_UP.index(k) if sx > 0 else X_DOWN.index(k)
                moved = shift_x(
                    moved, lambda: r_v[k, before, :], lambda: r_v[k, after, :], sx, halo_row
                )
            moved = shift_y(moved, sy)
            if sx or sy:
                moved = jnp.where(blocked[sx, sy], own[OPPOSITE[k]], moved)
            result = jnp.where(active, moved, f_v[k, at, :])
            if k in Y_ALL:
                partial[Y_ALL.index(k), at, :] = result
            else:
                stage[REST.index(k), at, :] = result
        return carry

    lax.fori_loop(0, TILES, tile, 0)
    copies = [
        pltpu.make_async_copy(stage.at[n], out_hbm.at[k], sems.at[n]) for n, k in enumerate(REST)
    ]
    for copy in copies:
        copy.start()
    for copy in copies:
        copy.wait()


def patch_kernel(first_ref, far_ref, second_ref, y_pre, partial, started, out_hbm, stage, sems):
    del started
    x, y, n_by = lax.axis_index("bx"), lax.axis_index("by"), lax.axis_size("by")
    even = lax.rem(y, 2) == 0
    seam = jnp.logical_or(y == 0, y == n_by // 2 - 1)
    ahead = jnp.logical_or(
        jnp.logical_and(x < lax.axis_size("bx") // 2, seam), jnp.logical_and(x == 0, y == 1)
    )
    near, far = jnp.where(ahead, first_ref[...], second_ref[...]), far_ref[...]
    below, above = jnp.where(even, far, near), jnp.where(even, near, far)
    flags = iota(0) >= 5
    free = [
        jnp.where(flags, jnp.where(message == 0.0, y_pre[slab], 0.0), message)
        for message, slab in ((below, 2), (above, 3))
    ]
    turned = jnp.transpose(
        jnp.concatenate(free + [jnp.zeros((SIDE - 16, SIDE), F32)], axis=0)
    )
    lane = lax.broadcasted_iota(jnp.int32, (SIDE, SIDE), 1)
    copies = []
    for n, k in enumerate(Y_ALL):
        side, which = n // 5, n % 5
        value = turned[:, side * 8 + which : side * 8 + which + 1]
        flag = side * 8 + FLAG_ROW[which]
        take = jnp.logical_and(
            lane == (0 if side == 0 else SIDE - 1), turned[:, flag : flag + 1] != 0.0
        )
        stage[n] = jnp.where(take, value, partial[n])
        copies.append(pltpu.make_async_copy(stage.at[n], out_hbm.at[k], sems.at[n]))
        copies[-1].start()
    for copy in copies:
        copy.wait()


def shape(*dims):
    return jax.ShapeDtypeStruct(dims, F32)


def in_vmem(*dims):
    return pltpu.VMEM(dims, F32)


def keep(x):
    return pltpu.with_memory_space_constraint(x, pltpu.VMEM)


def stay(x):
    return pltpu.with_memory_space_constraint(x, pltpu.HBM)


def pairs_of(first, last):
    pairs = []
    for low in range(first, last, 2):
        pairs += [(low, low + 1), (low + 1, low)]
    return pairs


def wrap_pairs(count):
    return [(count - 1, 0), (0, count - 1)]


def near_pairs(n_bx, n_by):
    ahead, rest = [], []
    for x in range(n_bx):
        for source, target in pairs_of(0, n_by):
            early = x < n_bx // 2 and target in (0, n_by // 2 - 1)
            pair = (x * n_by + source, x * n_by + target)
            (ahead if early or (x == 0 and target == 1) else rest).append(pair)
    return ahead, rest


def local(n_bx, n_by, populations, solid_mask, pore_list, pore_count):
    vmem = pl.BlockSpec(memory_space=pltpu.VMEM)
    smem = pl.BlockSpec(memory_space=pltpu.SMEM)
    hbm = pl.BlockSpec(memory_space=pltpu.HBM)
    anywhere = pl.BlockSpec(memory_space=pl.ANY)
    params = pltpu.CompilerParams(vmem_limit_bytes=24 * 2**20)
    plane = (SIDE, SIDE)
    f = populations.reshape(19, *plane)
    count, listed = pore_count.T, pore_list
    message = in_vmem(8, SIDE)
    collided = (in_vmem(19, *plane), in_vmem(*plane), in_vmem(*plane), in_vmem(4, 8, SIDE))
    chip_msg, off_msg, f_v, mask_v, *begun = pl.pallas_call(
        rim_kernel,
        out_shape=(message, message, in_vmem(19, *plane), pltpu.VMEM(plane, jnp.int32)) + collided,
        in_specs=[hbm] * 4,
        out_specs=[vmem] * 8,
        scratch_shapes=[
            pltpu.VMEM((2, 19, 8, SIDE), F32), pltpu.VMEM((2, 8, SIDE), jnp.int32),
            pltpu.SMEM((1, n_bx), jnp.int32), pltpu.SMEM((1, 1, 4), jnp.int32),
            pltpu.VMEM(plane, F32), pltpu.SemaphoreType.DMA((7 + CHUNKS,)),
        ],
        compiler_params=params,
        name="rim",
    )(stay(count), stay(listed), stay(f), stay(solid_mask.reshape(plane)))

    chip = lax.ppermute(chip_msg, "bx", pairs_of(0, n_bx))
    off = lax.ppermute(off_msg, "bx", pairs_of(1, n_bx - 1) + wrap_pairs(n_bx))

    r_v, solid_v, active_v, y_pre = pl.pallas_call(
        collide_kernel,
        out_shape=collided,
        in_specs=[smem] * 2 + [vmem] * 6,
        out_specs=[vmem] * 4,
        scratch_shapes=[pltpu.VMEM(plane, F32)],
        input_output_aliases={4: 0, 5: 1, 6: 2, 7: 3},
        compiler_params=params,
        cost_estimate=pl.CostEstimate(
            flops=8_000_000, bytes_accessed=4_000_000, transcendentals=0
        ),
        name="collide",
    )(count, listed, keep(f_v), keep(mask_v), *(keep(x) for x in begun))

    first_msg, far_msg, second_msg = pl.pallas_call(
        corner_kernel,
        out_shape=(message,) * 3,
        in_specs=[vmem] * 3,
        out_specs=[vmem] * 3,
        compiler_params=params,
        name="corner",
    )(keep(y_pre), keep(chip), keep(off))

    ahead, rest = near_pairs(n_bx, n_by)
    first = lax.ppermute(first_msg, ("bx", "by"), ahead)
    far = lax.ppermute(far_msg, "by", pairs_of(1, n_by - 1) + wrap_pairs(n_by))
    second = lax.ppermute(second_msg, ("bx", "by"), rest)

    out, partial = pl.pallas_call(
        stream_kernel,
        out_shape=(shape(19, *plane), in_vmem(10, *plane)),
        in_specs=[vmem] * 6,
        out_specs=[anywhere, vmem],
        scratch_shapes=[
            pltpu.VMEM((9, *plane), F32), pltpu.VMEM((2, 8, SIDE), F32),
            pltpu.SemaphoreType.DMA((9,)),
        ],
        compiler_params=params,
        cost_estimate=pl.CostEstimate(
            flops=8_000_000, bytes_accessed=4_000_000, transcendentals=0
        ),
        name="stream",
    )(keep(f_v), keep(r_v), keep(solid_v), keep(active_v), keep(chip), keep(off))

    out = pl.pallas_call(
        patch_kernel,
        out_shape=shape(19, *plane),
        in_specs=[vmem] * 5 + [anywhere],
        out_specs=anywhere,
        scratch_shapes=[pltpu.VMEM((10, *plane), F32), pltpu.SemaphoreType.DMA((10,))],
        input_output_aliases={5: 0},
        compiler_params=params,
        name="patch",
    )(keep(first), keep(far), keep(second), keep(y_pre), keep(partial), out)
    return out.reshape(19, 1, *plane)


def solution(mesh):
    placed = (P(None, None, "bx", "by"), P(None, "bx", "by"), P("bx", "by", None), P(None, "by"))
    return jax.shard_map(
        functools.partial(local, mesh.shape["bx"], mesh.shape["by"]),
        mesh=mesh,
        in_specs=placed,
        out_specs=P(None, None, "bx", "by"),
        check_vma=False,
    )
```

```python
import functools

import jax
import jax.numpy as jnp
from jax import lax
from jax.experimental import pallas as pl
from jax.experimental.pallas import tpu as pltpu
from jax.sharding import PartitionSpec as P

F32 = jnp.float32
SIDE = 128
TILES = SIDE // 8
CHUNKS = 2

PAIRS = (
    (1, 2, (1, 0, 0)),
    (3, 4, (0, 1, 0)),
    (5, 6, (0, 0, 1)),
    (7, 8, (1, 1, 0)),
    (9, 10, (1, -1, 0)),
    (11, 12, (1, 0, 1)),
    (13, 14, (1, 0, -1)),
    (15, 16, (0, 1, 1)),
    (17, 18, (0, 1, -1)),
)
VELOCITY = {0: (0, 0, 0)}
OPPOSITE = {0: 0}
for _k, _o, _c in PAIRS:
    VELOCITY[_k], VELOCITY[_o] = _c, tuple(-v for v in _c)
    OPPOSITE[_k], OPPOSITE[_o] = _o, _k
OMEGA_PLUS = 1.0 / 0.8
OMEGA_MINUS = 1.0 / (0.1875 / 0.3 + 0.5)

X_UP, X_DOWN = (1, 7, 9, 11, 13), (2, 8, 10, 12, 14)
Y_UP, Y_DOWN = (3, 7, 10, 15, 17), (4, 8, 9, 16, 18)
Y_ALL = Y_UP + Y_DOWN
REST = tuple(k for k in range(19) if k not in Y_ALL)
RUNS = ((0, 3), (5, 2), (11, 4))
PARTS = 4
FLAG_ROW = (5, 6, 7, 5, 5)


def iota(axis):
    return lax.broadcasted_iota(jnp.int32, (8, SIDE), axis)


def relax(f):
    total = {p: f[k] + f[o] for p, (k, o, _) in enumerate(PAIRS)}
    diff = {p: f[k] - f[o] for p, (k, o, _) in enumerate(PAIRS)}
    density = ((total[0] + total[1]) + (total[2] + total[3])) + (
        (total[4] + total[5]) + (total[6] + total[7])
    )
    density = density + (total[8] + f[0])
    jx = (diff[0] + diff[3]) + (diff[4] + diff[5]) + diff[6]
    jy = (diff[1] + diff[3]) + (diff[7] - diff[4]) + diff[8]
    jz = (diff[2] + diff[5]) + (diff[7] - diff[6]) - diff[8]
    inverse = 1.0 / density
    speed = (jx * inverse, jy * inverse, jz * inverse)
    square = speed[0] * speed[0] + speed[1] * speed[1] + speed[2] * speed[2]
    base = 1.0 - 1.5 * square
    out = {0: f[0] - OMEGA_PLUS * (f[0] - (density * base) * (1.0 / 3.0))}
    for p, (k, o, c) in enumerate(PAIRS):
        weight = 1.0 / 18.0 if p < 3 else 1.0 / 36.0
        dotted = None
        for axis in range(3):
            if c[axis]:
                term = speed[axis] if c[axis] > 0 else -speed[axis]
                dotted = term if dotted is None else dotted + term
        scaled = density * weight
        even = 0.5 * total[p] - scaled * (base + 4.5 * (dotted * dotted))
        odd = 0.5 * diff[p] - scaled * (3.0 * dotted)
        out[k] = f[k] - OMEGA_PLUS * even - OMEGA_MINUS * odd
        out[o] = f[o] - OMEGA_PLUS * even + OMEGA_MINUS * odd
    return out


def is_early():
    position = lax.axis_index("bx") + lax.axis_index("by")
    return jnp.logical_and(
        jnp.logical_and(
            lax.axis_index("bx") < lax.axis_size("bx") // 2,
            lax.axis_index("by") < lax.axis_size("by") // 2,
        ),
        position > 0,
    )


def live_blocks(count_ref, list_ref):
    count = count_ref[0, lax.axis_index("bx")]
    live = []
    for b in range(4):
        hit = jnp.int32(0)
        for s in range(4):
            found = jnp.logical_and(s < count, list_ref[0, 0, s] == b)
            hit = jnp.where(found, jnp.int32(1), hit)
        live.append(hit)
    return live


def collide_block(
    f_hbm, m_hbm, live_v, f_v, r_v, solid_v, active_v, y_pre, mask_v, columns, sems
):
    lane, row = iota(1), iota(0)
    rows = SIDE // CHUNKS
    copies = [pltpu.make_async_copy(m_hbm, mask_v, sems.at[CHUNKS])]
    for c in range(CHUNKS):
        part = pl.ds(c * rows, rows)
        copies.append(
            pltpu.make_async_copy(f_hbm.at[:, part, :], f_v.at[:, part, :], sems.at[c])
        )
    for copy in copies:
        copy.start()
    copies[0].wait()

    def tile(t, carry):
        at = pl.ds(pl.multiple_of(t * 8, 8), 8)
        is_live = live_v[t // (TILES // 2)] != 0.0
        f = [f_v[k, at, :] for k in range(19)]
        out = relax(f)
        out = [jnp.where(is_live, out[k], f[k]) for k in range(19)]
        for k in range(19):
            r_v[k, at, :] = out[k]
        solid = mask_v[at, :].astype(F32)
        solid_v[at, :] = solid
        active_v[at, :] = jnp.where(jnp.logical_and(is_live, solid == 0.0), 1.0, 0.0)
        packed = jnp.zeros((8, SIDE), F32)
        for start, edge, pops in ((0, SIDE - 1, Y_UP), (8, 0, Y_DOWN)):
            for n, k in enumerate(pops):
                packed = jnp.where(lane == start + n, out[k][:, edge : edge + 1], packed)
            flags = jnp.logical_and(lane >= start + 5, lane < start + 8)
            packed = jnp.where(flags, solid[:, edge : edge + 1], packed)
        columns[at, :] = packed
        return carry

    for c in range(CHUNKS):
        copies[1 + c].wait()
        lax.fori_loop(c * (rows // 8), (c + 1) * (rows // 8), tile, 0, unroll=rows // 8)

    turned = jnp.transpose(columns[...])
    high, low = turned[0:8, :], turned[8:16, :]
    fore = jnp.logical_or(row == 1, row == 6)
    back = jnp.logical_or(row == 2, row == 7)
    y_pre[0] = jnp.where(
        fore, pltpu.roll(high, 1, 1), jnp.where(back, pltpu.roll(high, SIDE - 1, 1), high)
    )
    y_pre[1] = jnp.where(
        fore, pltpu.roll(low, SIDE - 1, 1), jnp.where(back, pltpu.roll(low, 1, 1), low)
    )
    for slab, flags in ((2, low), (3, high)):
        free = jnp.broadcast_to(flags[5:6, :], (8, SIDE)) == 0.0
        y_pre[slab] = jnp.where(free, live_v[slab], 0.0)


def rim_kernel(
    count_hbm, list_hbm, f_hbm, m_hbm,
    chip_msg, off_msg, live_v, f_v, r_v, solid_v, active_v, y_pre,
    edge_f, edge_m, count_ref, list_ref, mask_v, columns, sems, edge_sems,
):
    ends = (pl.ds(SIDE - 8, 8), pl.ds(0, 8))
    pairs = [(count_hbm, count_ref), (list_hbm, list_ref)]
    for n, end in enumerate(ends):
        pairs += [(m_hbm.at[end, :], edge_m.at[n]), (f_hbm.at[:, end, :], edge_f.at[n])]
    copies = [pltpu.make_async_copy(s, t, edge_sems.at[n]) for n, (s, t) in enumerate(pairs)]
    for copy in copies:
        copy.start()
    for copy in copies:
        copy.wait()
    live = live_blocks(count_ref, list_ref)
    lane = iota(1)
    for n, (left, right) in enumerate(((0, 1), (2, 3), (0, 2), (1, 3))):
        live_v[n] = jnp.where(lane < SIDE // 2, live[left], live[right]).astype(F32)
    messages = []
    for n, (pops, inner) in enumerate(((X_UP, 7), (X_DOWN, 0))):
        f = [edge_f[n, k] for k in range(19)]
        out = relax(f)
        is_live = live_v[1 - n] != 0.0
        solid = edge_m[n].astype(F32)
        rows = [jnp.where(is_live, out[k], f[k])[inner : inner + 1, :] for k in pops]
        rows += [solid[inner : inner + 1, :]] * 3
        messages.append(jnp.concatenate(rows, axis=0))
    up, down = messages
    even = lax.rem(lax.axis_index("bx"), 2) == 0
    chip_msg[...] = jnp.where(even, up, down)
    off_msg[...] = jnp.where(even, down, up)

    @pl.when(is_early())
    def _():
        collide_block(
            f_hbm, m_hbm, live_v, f_v, r_v, solid_v, active_v, y_pre, mask_v, columns, sems
        )


def collide_kernel(
    f_hbm, m_hbm, live_v, f_in, r_in, solid_in, active_in, y_in,
    f_v, r_v, solid_v, active_v, y_pre, mask_v, columns, sems,
):
    del f_in, r_in, solid_in, active_in, y_in

    @pl.when(jnp.logical_not(is_early()))
    def _():
        collide_block(
            f_hbm, m_hbm, live_v, f_v, r_v, solid_v, active_v, y_pre, mask_v, columns, sems
        )


def halos(chip_ref, off_ref):
    parity = lax.rem(lax.axis_index("bx"), 2)
    chip, off = chip_ref[...], off_ref[...]
    return jnp.where(parity == 0, off, chip), jnp.where(parity == 0, chip, off)


def corner_kernel(y_pre, chip_ref, off_ref, first_msg, far_msg, second_msg):
    low, high = halos(chip_ref, off_ref)
    lane, row = iota(1), iota(0)
    fore = jnp.logical_or(row == 1, row == 6)
    back = jnp.logical_or(row == 2, row == 7)
    first, last = lane == 0, lane == SIDE - 1
    up = jnp.where(jnp.logical_and(fore, first), pltpu.roll(low, 1, 1), y_pre[0])
    up = jnp.where(jnp.logical_and(back, last), high, up)
    down = jnp.where(jnp.logical_and(fore, last), pltpu.roll(high, SIDE - 1, 1), y_pre[1])
    down = jnp.where(jnp.logical_and(back, first), low, down)
    even = lax.rem(lax.axis_index("by"), 2) == 0
    first_msg[...] = jnp.where(even, up, down)
    far_msg[...] = jnp.where(even, down, up)
    second_msg[...] = jnp.where(even, up, down)


def stream_kernel(
    f_v, r_v, solid_v, active_v, chip_ref, off_ref, out_hbm, partial, stage, edges, sems
):
    low, high = halos(chip_ref, off_ref)
    edges[0], edges[1] = low, high
    lane, row = iota(1), iota(0)
    top, bottom = row == 0, row == 7
    first, last = lane == 0, lane == SIDE - 1

    def tile(t, carry):
        at = pl.ds(pl.multiple_of(t * 8, 8), 8)
        before = pl.ds(jnp.maximum(t * 8 - 1, 0), 1)
        after = pl.ds(jnp.minimum(t * 8 + 8, SIDE - 1), 1)

        def shift_x(block, row_before, row_after, step, halo_row):
            if step == 0:
                return block
            if step > 0:
                edge = jnp.where(t == 0, edges[0, halo_row : halo_row + 1, :], row_before())
                return jnp.where(top, edge, pltpu.roll(block, 1, 0))
            edge = jnp.where(t == TILES - 1, edges[1, halo_row : halo_row + 1, :], row_after())
            return jnp.where(bottom, edge, pltpu.roll(block, 7, 0))

        def shift_y(block, step):
            if step == 0:
                return block
            return pltpu.roll(block, 1 if step > 0 else SIDE - 1, 1)

        solid = solid_v[at, :]
        active = active_v[at, :] != 0.0
        blocked = {}
        for sx in (-1, 0, 1):
            moved = shift_x(
                solid, lambda: solid_v[before, :], lambda: solid_v[after, :], sx, 5
            )
            for sy in (-1, 0, 1):
                if sx or sy:
                    hit = shift_y(moved, sy) != 0.0
                    if sy:
                        hit = jnp.logical_or(hit, first if sy > 0 else last)
                    blocked[sx, sy] = hit
        own = [r_v[k, at, :] for k in range(19)]
        for k in range(19):
            sx, sy, _ = VELOCITY[k]
            moved = own[k]
            if sx:
                halo_row = X_UP.index(k) if sx > 0 else X_DOWN.index(k)
                moved = shift_x(
                    moved, lambda: r_v[k, before, :], lambda: r_v[k, after, :], sx, halo_row
                )
            moved = shift_y(moved, sy)
            if sx or sy:
                moved = jnp.where(blocked[sx, sy], own[OPPOSITE[k]], moved)
            result = jnp.where(active, moved, f_v[k, at, :])
            if k in Y_ALL:
                partial[Y_ALL.index(k), at, :] = result
            else:
                stage[REST.index(k), at, :] = result
        return carry

    copies = []
    for part in range(PARTS):
        tiles = TILES // PARTS
        lax.fori_loop(part * tiles, (part + 1) * tiles, tile, 0, unroll=tiles)
        rows = pl.ds(part * tiles * 8, tiles * 8)
        for n, (start, count) in enumerate(RUNS):
            first = REST.index(start)
            copy = pltpu.make_async_copy(
                stage.at[first : first + count, rows, :],
                out_hbm.at[start : start + count, rows, :],
                sems.at[part * len(RUNS) + n],
            )
            copy.start()
            copies.append(copy)
    for copy in copies:
        copy.wait()


def patch_kernel(first_ref, far_ref, second_ref, y_pre, partial, started, out_hbm, stage, sems):
    del started
    x, y, n_by = lax.axis_index("bx"), lax.axis_index("by"), lax.axis_size("by")
    even = lax.rem(y, 2) == 0
    seam = jnp.logical_or(y == 0, y == n_by // 2 - 1)
    ahead = jnp.logical_or(
        jnp.logical_and(x < lax.axis_size("bx") // 2, seam), jnp.logical_and(x == 0, y == 1)
    )
    near, far = jnp.where(ahead, first_ref[...], second_ref[...]), far_ref[...]
    below, above = jnp.where(even, far, near), jnp.where(even, near, far)
    flags = iota(0) >= 5
    free = [
        jnp.where(flags, jnp.where(message == 0.0, y_pre[slab], 0.0), message)
        for message, slab in ((below, 2), (above, 3))
    ]
    turned = jnp.transpose(
        jnp.concatenate(free + [jnp.zeros((SIDE - 16, SIDE), F32)], axis=0)
    )
    lane = lax.broadcasted_iota(jnp.int32, (SIDE, SIDE), 1)
    copies = []
    for n, k in enumerate(Y_ALL):
        side, which = n // 5, n % 5
        value = turned[:, side * 8 + which : side * 8 + which + 1]
        flag = side * 8 + FLAG_ROW[which]
        take = jnp.logical_and(
            lane == (0 if side == 0 else SIDE - 1), turned[:, flag : flag + 1] != 0.0
        )
        stage[n] = jnp.where(take, value, partial[n])
        copies.append(pltpu.make_async_copy(stage.at[n], out_hbm.at[k], sems.at[n]))
        copies[-1].start()
    for copy in copies:
        copy.wait()


def shape(*dims):
    return jax.ShapeDtypeStruct(dims, F32)


def in_vmem(*dims):
    return pltpu.VMEM(dims, F32)


def keep(x):
    return pltpu.with_memory_space_constraint(x, pltpu.VMEM)


def stay(x):
    return pltpu.with_memory_space_constraint(x, pltpu.HBM)


def pairs_of(first, last):
    pairs = []
    for low in range(first, last, 2):
        pairs += [(low, low + 1), (low + 1, low)]
    return pairs


def wrap_pairs(count):
    return [(count - 1, 0), (0, count - 1)]


def near_pairs(n_bx, n_by):
    ahead, rest = [], []
    for x in range(n_bx):
        for source, target in pairs_of(0, n_by):
            early = x < n_bx // 2 and target in (0, n_by // 2 - 1)
            pair = (x * n_by + source, x * n_by + target)
            (ahead if early or (x == 0 and target == 1) else rest).append(pair)
    return ahead, rest


def local(n_bx, n_by, populations, solid_mask, pore_list, pore_count):
    vmem = pl.BlockSpec(memory_space=pltpu.VMEM)
    hbm = pl.BlockSpec(memory_space=pltpu.HBM)
    anywhere = pl.BlockSpec(memory_space=pl.ANY)
    params = pltpu.CompilerParams(vmem_limit_bytes=24 * 2**20)
    plane = (SIDE, SIDE)
    f, mask = stay(populations.reshape(19, *plane)), stay(solid_mask.reshape(plane))
    message = in_vmem(8, SIDE)
    collided = (
        in_vmem(19, *plane), in_vmem(19, *plane), in_vmem(*plane), in_vmem(*plane),
        in_vmem(4, 8, SIDE),
    )
    work = [
        pltpu.VMEM(plane, jnp.int32), pltpu.VMEM(plane, F32),
        pltpu.SemaphoreType.DMA((CHUNKS + 1,)),
    ]
    chip_msg, off_msg, live_v, *begun = pl.pallas_call(
        rim_kernel,
        out_shape=(message, message, in_vmem(4, 8, SIDE)) + collided,
        in_specs=[hbm] * 4,
        out_specs=[vmem] * 8,
        scratch_shapes=[
            pltpu.VMEM((2, 19, 8, SIDE), F32), pltpu.VMEM((2, 8, SIDE), jnp.int32),
            pltpu.SMEM((1, n_bx), jnp.int32), pltpu.SMEM((1, 1, 4), jnp.int32),
            *work, pltpu.SemaphoreType.DMA((6,)),
        ],
        compiler_params=params,
        name="rim",
    )(stay(pore_count.T), stay(pore_list), f, mask)

    chip = lax.ppermute(chip_msg, "bx", pairs_of(0, n_bx))
    off = lax.ppermute(off_msg, "bx", pairs_of(1, n_bx - 1) + wrap_pairs(n_bx))

    f_v, r_v, solid_v, active_v, y_pre = pl.pallas_call(
        collide_kernel,
        out_shape=collided,
        in_specs=[hbm] * 2 + [vmem] * 6,
        out_specs=[vmem] * 5,
        scratch_shapes=work,
        input_output_aliases={3: 0, 4: 1, 5: 2, 6: 3, 7: 4},
        compiler_params=params,
        cost_estimate=pl.CostEstimate(
            flops=8_000_000, bytes_accessed=4_000_000, transcendentals=0
        ),
        name="collide",
    )(f, mask, keep(live_v), *(keep(x) for x in begun))

    first_msg, far_msg, second_msg = pl.pallas_call(
        corner_kernel,
        out_shape=(message,) * 3,
        in_specs=[vmem] * 3,
        out_specs=[vmem] * 3,
        compiler_params=params,
        name="corner",
    )(keep(y_pre), keep(chip), keep(off))

    ahead, rest = near_pairs(n_bx, n_by)
    first = lax.ppermute(first_msg, ("bx", "by"), ahead)
    far = lax.ppermute(far_msg, "by", pairs_of(1, n_by - 1) + wrap_pairs(n_by))
    second = lax.ppermute(second_msg, ("bx", "by"), rest)

    out, partial = pl.pallas_call(
        stream_kernel,
        out_shape=(shape(19, *plane), in_vmem(10, *plane)),
        in_specs=[vmem] * 6,
        out_specs=[anywhere, vmem],
        scratch_shapes=[
            pltpu.VMEM((9, *plane), F32), pltpu.VMEM((2, 8, SIDE), F32),
            pltpu.SemaphoreType.DMA((PARTS * len(RUNS),)),
        ],
        compiler_params=params,
        cost_estimate=pl.CostEstimate(
            flops=8_000_000, bytes_accessed=4_000_000, transcendentals=0
        ),
        name="stream",
    )(keep(f_v), keep(r_v), keep(solid_v), keep(active_v), keep(chip), keep(off))

    out = pl.pallas_call(
        patch_kernel,
        out_shape=shape(19, *plane),
        in_specs=[vmem] * 5 + [anywhere],
        out_specs=anywhere,
        scratch_shapes=[pltpu.VMEM((10, *plane), F32), pltpu.SemaphoreType.DMA((10,))],
        input_output_aliases={5: 0},
        compiler_params=params,
        name="patch",
    )(keep(first), keep(far), keep(second), keep(y_pre), keep(partial), out)
    return out.reshape(19, 1, *plane)


def solution(mesh):
    placed = (P(None, None, "bx", "by"), P(None, "bx", "by"), P("bx", "by", None), P(None, "by"))
    return jax.shard_map(
        functools.partial(local, mesh.shape["bx"], mesh.shape["by"]),
        mesh=mesh,
        in_specs=placed,
        out_specs=P(None, None, "bx", "by"),
        check_vma=False,
    )
```

```python
import functools

import jax
import jax.numpy as jnp
import numpy as np
from jax import lax
from jax.experimental import pallas as pl
from jax.experimental.pallas import tpu as pltpu
from jax.sharding import PartitionSpec as P

F32 = jnp.float32
SIDE = 128
TILES = SIDE // 8
CHUNKS = 2
X_SLOTS, Y_SLOTS = 3, 3

PAIRS = (
    (1, 2, (1, 0, 0)),
    (3, 4, (0, 1, 0)),
    (5, 6, (0, 0, 1)),
    (7, 8, (1, 1, 0)),
    (9, 10, (1, -1, 0)),
    (11, 12, (1, 0, 1)),
    (13, 14, (1, 0, -1)),
    (15, 16, (0, 1, 1)),
    (17, 18, (0, 1, -1)),
)
VELOCITY = {0: (0, 0, 0)}
OPPOSITE = {0: 0}
for _k, _o, _c in PAIRS:
    VELOCITY[_k], VELOCITY[_o] = _c, tuple(-v for v in _c)
    OPPOSITE[_k], OPPOSITE[_o] = _o, _k
OMEGA_PLUS = 1.0 / 0.8
OMEGA_MINUS = 1.0 / (0.1875 / 0.3 + 0.5)

X_UP, X_DOWN = (1, 7, 9, 11, 13), (2, 8, 10, 12, 14)
Y_UP, Y_DOWN = (3, 7, 10, 15, 17), (4, 8, 9, 16, 18)
Y_ALL = Y_UP + Y_DOWN
REST = tuple(k for k in range(19) if k not in Y_ALL)
RUNS = ((0, 3), (5, 2), (11, 4))
PARTS = 4
FLAG_ROW = (5, 6, 7, 5, 5)


def iota(axis):
    return lax.broadcasted_iota(jnp.int32, (8, SIDE), axis)


def relax(f):
    total = {p: f[k] + f[o] for p, (k, o, _) in enumerate(PAIRS)}
    diff = {p: f[k] - f[o] for p, (k, o, _) in enumerate(PAIRS)}
    density = ((total[0] + total[1]) + (total[2] + total[3])) + (
        (total[4] + total[5]) + (total[6] + total[7])
    )
    density = density + (total[8] + f[0])
    jx = (diff[0] + diff[3]) + (diff[4] + diff[5]) + diff[6]
    jy = (diff[1] + diff[3]) + (diff[7] - diff[4]) + diff[8]
    jz = (diff[2] + diff[5]) + (diff[7] - diff[6]) - diff[8]
    inverse = 1.0 / density
    speed = (jx * inverse, jy * inverse, jz * inverse)
    square = speed[0] * speed[0] + speed[1] * speed[1] + speed[2] * speed[2]
    base = 1.0 - 1.5 * square
    out = {0: f[0] - OMEGA_PLUS * (f[0] - (density * base) * (1.0 / 3.0))}
    for p, (k, o, c) in enumerate(PAIRS):
        weight = 1.0 / 18.0 if p < 3 else 1.0 / 36.0
        dotted = None
        for axis in range(3):
            if c[axis]:
                term = speed[axis] if c[axis] > 0 else -speed[axis]
                dotted = term if dotted is None else dotted + term
        scaled = density * weight
        even = 0.5 * total[p] - scaled * (base + 4.5 * (dotted * dotted))
        odd = 0.5 * diff[p] - scaled * (3.0 * dotted)
        out[k] = f[k] - OMEGA_PLUS * even - OMEGA_MINUS * odd
        out[o] = f[o] - OMEGA_PLUS * even + OMEGA_MINUS * odd
    return out


def is_early():
    position = lax.axis_index("bx") + lax.axis_index("by")
    return jnp.logical_and(
        jnp.logical_and(
            lax.axis_index("bx") < lax.axis_size("bx") // 2,
            lax.axis_index("by") < lax.axis_size("by") // 2,
        ),
        position > 0,
    )


def live_blocks(count_ref, list_ref):
    count = count_ref[0, lax.axis_index("bx")]
    live = []
    for b in range(4):
        hit = jnp.int32(0)
        for s in range(4):
            found = jnp.logical_and(s < count, list_ref[0, 0, s] == b)
            hit = jnp.where(found, jnp.int32(1), hit)
        live.append(hit)
    return live


def collide_block(
    f_hbm, m_hbm, live_v, f_v, r_v, solid_v, active_v, y_pre, mask_v, columns, sems
):
    lane, row = iota(1), iota(0)
    rows = SIDE // CHUNKS
    copies = [pltpu.make_async_copy(m_hbm, mask_v, sems.at[CHUNKS])]
    for c in range(CHUNKS):
        part = pl.ds(c * rows, rows)
        copies.append(
            pltpu.make_async_copy(f_hbm.at[:, part, :], f_v.at[:, part, :], sems.at[c])
        )
    for copy in copies:
        copy.start()
    copies[0].wait()

    def tile(t, carry):
        at = pl.ds(pl.multiple_of(t * 8, 8), 8)
        is_live = live_v[t // (TILES // 2)] != 0.0
        f = [f_v[k, at, :] for k in range(19)]
        out = relax(f)
        out = [jnp.where(is_live, out[k], f[k]) for k in range(19)]
        for k in range(19):
            r_v[k, at, :] = out[k]
        solid = mask_v[at, :].astype(F32)
        solid_v[at, :] = solid
        active_v[at, :] = jnp.where(jnp.logical_and(is_live, solid == 0.0), 1.0, 0.0)
        packed = jnp.zeros((8, SIDE), F32)
        for start, edge, pops in ((0, SIDE - 1, Y_UP), (8, 0, Y_DOWN)):
            for n, k in enumerate(pops):
                packed = jnp.where(lane == start + n, out[k][:, edge : edge + 1], packed)
            flags = jnp.logical_and(lane >= start + 5, lane < start + 8)
            packed = jnp.where(flags, solid[:, edge : edge + 1], packed)
        columns[at, :] = packed
        return carry

    for c in range(CHUNKS):
        copies[1 + c].wait()
        lax.fori_loop(c * (rows // 8), (c + 1) * (rows // 8), tile, 0, unroll=rows // 8)

    turned = jnp.transpose(columns[...])
    high, low = turned[0:8, :], turned[8:16, :]
    fore = jnp.logical_or(row == 1, row == 6)
    back = jnp.logical_or(row == 2, row == 7)
    y_pre[0] = jnp.where(
        fore, pltpu.roll(high, 1, 1), jnp.where(back, pltpu.roll(high, SIDE - 1, 1), high)
    )
    y_pre[1] = jnp.where(
        fore, pltpu.roll(low, SIDE - 1, 1), jnp.where(back, pltpu.roll(low, 1, 1), low)
    )
    for slab, flags in ((2, low), (3, high)):
        free = jnp.broadcast_to(flags[5:6, :], (8, SIDE)) == 0.0
        y_pre[slab] = jnp.where(free, live_v[slab], 0.0)


def rim_kernel(
    count_hbm, list_hbm, plan_hbm, f_hbm, m_hbm, *refs,
):
    x_msgs, refs = refs[:X_SLOTS], refs[X_SLOTS:]
    (
        picks, live_v, f_v, r_v, solid_v, active_v, y_pre,
        edge_f, edge_m, count_ref, list_ref, plan_ref, mask_v, columns, sems, edge_sems,
    ) = refs
    ends = (pl.ds(SIDE - 8, 8), pl.ds(0, 8))
    pairs = [(count_hbm, count_ref), (list_hbm, list_ref), (plan_hbm, plan_ref)]
    for n, end in enumerate(ends):
        pairs += [(m_hbm.at[end, :], edge_m.at[n]), (f_hbm.at[:, end, :], edge_f.at[n])]
    copies = [pltpu.make_async_copy(s, t, edge_sems.at[n]) for n, (s, t) in enumerate(pairs)]
    for copy in copies:
        copy.start()
    for copy in copies:
        copy.wait()
    live = live_blocks(count_ref, list_ref)
    lane = iota(1)
    for n, (left, right) in enumerate(((0, 1), (2, 3), (0, 2), (1, 3))):
        live_v[n] = jnp.where(lane < SIDE // 2, live[left], live[right]).astype(F32)
    messages = []
    for n, (pops, inner) in enumerate(((X_UP, 7), (X_DOWN, 0))):
        f = [edge_f[n, k] for k in range(19)]
        out = relax(f)
        is_live = live_v[1 - n] != 0.0
        solid = edge_m[n].astype(F32)
        rows = [jnp.where(is_live, out[k], f[k])[inner : inner + 1, :] for k in pops]
        rows += [solid[inner : inner + 1, :]] * 3
        messages.append(jnp.concatenate(rows, axis=0))
    up, down = messages
    code = plan_ref[0, lax.axis_index("bx") * lax.axis_size("by") + lax.axis_index("by")]
    for n in range(4):
        picks[n] = jnp.broadcast_to(lax.rem(code >> (2 * n), 4), (8, SIDE)).astype(F32)
    for n in range(X_SLOTS):
        x_msgs[n][...] = jnp.where(lax.rem(code >> (8 + n), 2) == 1, up, down)
    for n in range(Y_SLOTS):
        bit = lax.rem(code >> (8 + X_SLOTS + n), 2)
        picks[4 + n] = jnp.broadcast_to(bit, (8, SIDE)).astype(F32)

    @pl.when(is_early())
    def _():
        collide_block(
            f_hbm, m_hbm, live_v, f_v, r_v, solid_v, active_v, y_pre, mask_v, columns, sems
        )


def collide_kernel(
    f_hbm, m_hbm, live_v, f_in, r_in, solid_in, active_in, y_in,
    f_v, r_v, solid_v, active_v, y_pre, mask_v, columns, sems,
):
    del f_in, r_in, solid_in, active_in, y_in

    @pl.when(jnp.logical_not(is_early()))
    def _():
        collide_block(
            f_hbm, m_hbm, live_v, f_v, r_v, solid_v, active_v, y_pre, mask_v, columns, sems
        )


def chosen(pick, refs):
    taken = refs[0][...]
    for n, ref in enumerate(refs[1:], 1):
        taken = jnp.where(pick == float(n), ref[...], taken)
    return taken


def corner_kernel(y_pre, picks, *refs):
    halos, y_msgs = refs[:X_SLOTS], refs[X_SLOTS:]
    low, high = chosen(picks[0], halos), chosen(picks[1], halos)
    lane, row = iota(1), iota(0)
    fore = jnp.logical_or(row == 1, row == 6)
    back = jnp.logical_or(row == 2, row == 7)
    first, last = lane == 0, lane == SIDE - 1
    up = jnp.where(jnp.logical_and(fore, first), pltpu.roll(low, 1, 1), y_pre[0])
    up = jnp.where(jnp.logical_and(back, last), high, up)
    down = jnp.where(jnp.logical_and(fore, last), pltpu.roll(high, SIDE - 1, 1), y_pre[1])
    down = jnp.where(jnp.logical_and(back, first), low, down)
    for n, message in enumerate(y_msgs):
        message[...] = jnp.where(picks[4 + n] == 1.0, up, down)


def stream_kernel(
    f_v, r_v, solid_v, active_v, picks, *refs,
):
    halos, (out_hbm, partial, stage, edges, sems) = refs[:X_SLOTS], refs[X_SLOTS:]
    edges[0], edges[1] = chosen(picks[0], halos), chosen(picks[1], halos)
    lane, row = iota(1), iota(0)
    top, bottom = row == 0, row == 7
    first, last = lane == 0, lane == SIDE - 1

    def tile(t, carry):
        at = pl.ds(pl.multiple_of(t * 8, 8), 8)
        before = pl.ds(jnp.maximum(t * 8 - 1, 0), 1)
        after = pl.ds(jnp.minimum(t * 8 + 8, SIDE - 1), 1)

        def shift_x(block, row_before, row_after, step, halo_row):
            if step == 0:
                return block
            if step > 0:
                edge = jnp.where(t == 0, edges[0, halo_row : halo_row + 1, :], row_before())
                return jnp.where(top, edge, pltpu.roll(block, 1, 0))
            edge = jnp.where(t == TILES - 1, edges[1, halo_row : halo_row + 1, :], row_after())
            return jnp.where(bottom, edge, pltpu.roll(block, 7, 0))

        def shift_y(block, step):
            if step == 0:
                return block
            return pltpu.roll(block, 1 if step > 0 else SIDE - 1, 1)

        solid = solid_v[at, :]
        active = active_v[at, :] != 0.0
        blocked = {}
        for sx in (-1, 0, 1):
            moved = shift_x(
                solid, lambda: solid_v[before, :], lambda: solid_v[after, :], sx, 5
            )
            for sy in (-1, 0, 1):
                if sx or sy:
                    hit = shift_y(moved, sy) != 0.0
                    if sy:
                        hit = jnp.logical_or(hit, first if sy > 0 else last)
                    blocked[sx, sy] = hit
        own = [r_v[k, at, :] for k in range(19)]
        for k in range(19):
            sx, sy, _ = VELOCITY[k]
            moved = own[k]
            if sx:
                halo_row = X_UP.index(k) if sx > 0 else X_DOWN.index(k)
                moved = shift_x(
                    moved, lambda: r_v[k, before, :], lambda: r_v[k, after, :], sx, halo_row
                )
            moved = shift_y(moved, sy)
            if sx or sy:
                moved = jnp.where(blocked[sx, sy], own[OPPOSITE[k]], moved)
            result = jnp.where(active, moved, f_v[k, at, :])
            if k in Y_ALL:
                partial[Y_ALL.index(k), at, :] = result
            else:
                stage[REST.index(k), at, :] = result
        return carry

    copies = []
    for part in range(PARTS):
        tiles = TILES // PARTS
        lax.fori_loop(part * tiles, (part + 1) * tiles, tile, 0, unroll=tiles)
        rows = pl.ds(part * tiles * 8, tiles * 8)
        for n, (start, count) in enumerate(RUNS):
            first = REST.index(start)
            copy = pltpu.make_async_copy(
                stage.at[first : first + count, rows, :],
                out_hbm.at[start : start + count, rows, :],
                sems.at[part * len(RUNS) + n],
            )
            copy.start()
            copies.append(copy)
    for copy in copies:
        copy.wait()


def patch_kernel(y_pre, picks, partial, started, *refs):
    del started
    halos, (out_hbm, stage, sems) = refs[:Y_SLOTS], refs[Y_SLOTS:]
    below, above = chosen(picks[2], halos), chosen(picks[3], halos)
    flags = iota(0) >= 5
    free = [
        jnp.where(flags, jnp.where(message == 0.0, y_pre[slab], 0.0), message)
        for message, slab in ((below, 2), (above, 3))
    ]
    turned = jnp.transpose(
        jnp.concatenate(free + [jnp.zeros((SIDE - 16, SIDE), F32)], axis=0)
    )
    lane = lax.broadcasted_iota(jnp.int32, (SIDE, SIDE), 1)
    copies = []
    for n, k in enumerate(Y_ALL):
        side, which = n // 5, n % 5
        value = turned[:, side * 8 + which : side * 8 + which + 1]
        flag = side * 8 + FLAG_ROW[which]
        take = jnp.logical_and(
            lane == (0 if side == 0 else SIDE - 1), turned[:, flag : flag + 1] != 0.0
        )
        stage[n] = jnp.where(take, value, partial[n])
        copies.append(pltpu.make_async_copy(stage.at[n], out_hbm.at[k], sems.at[n]))
        copies[-1].start()
    for copy in copies:
        copy.wait()


def shape(*dims):
    return jax.ShapeDtypeStruct(dims, F32)


def in_vmem(*dims):
    return pltpu.VMEM(dims, F32)


def keep(x):
    return pltpu.with_memory_space_constraint(x, pltpu.VMEM)


def stay(x):
    return pltpu.with_memory_space_constraint(x, pltpu.HBM)


def slots(n_bx, n_by):
    chosen_slots = {}
    for x in range(n_bx):
        for y in range(n_by):
            if x % 2 == 0:
                slot = 1 if y == 0 else 2 if x == n_bx - 2 else 0
            else:
                slot = 1 if y else 2 if x == n_bx - 1 else 0
            chosen_slots["x", x, y, 1] = chosen_slots["x", (x + 1) % n_bx, y, -1] = slot
            up, down = (x, y, 1), (x, (y + 1) % n_by, -1)
            for source, target in ((up, y + 1), (down, y)):
                ahead = x < n_bx // 2 and target in (0, n_by // 2 - 1)
                chosen_slots["y", *source] = 1 if y % 2 else 0 if ahead else 2
            if x == 0 and (y < 4 or y >= n_by - 3):
                special = {0: 1, 1: 0, 2: 2, 3: 0, n_by - 3: 1, n_by - 2: 0, n_by - 1: 2}
                chosen_slots["y", *up] = chosen_slots["y", *down] = special[y]
    return chosen_slots


def plan(n_bx, n_by):
    chosen_slots = slots(n_bx, n_by)
    pairs = {"x": [[] for _ in range(X_SLOTS)], "y": [[] for _ in range(Y_SLOTS)]}
    codes = np.zeros((n_bx, n_by), np.int32)
    for (axis, x, y, step), slot in chosen_slots.items():
        to = ((x + step) % n_bx, y) if axis == "x" else (x, (y + step) % n_by)
        pairs[axis][slot].append((x * n_by + y, to[0] * n_by + to[1]))
        side = (0 if axis == "x" else 2) + (0 if step > 0 else 1)
        codes[to] += slot << (2 * side)
        if step > 0:
            codes[x, y] += 1 << (8 + slot + (0 if axis == "x" else X_SLOTS))
    for group in pairs["x"] + pairs["y"]:
        for end in zip(*group):
            assert len(set(end)) == len(end)
    return pairs, codes.reshape(1, -1)


def local(n_bx, n_by, populations, solid_mask, pore_list, pore_count):
    vmem = pl.BlockSpec(memory_space=pltpu.VMEM)
    hbm = pl.BlockSpec(memory_space=pltpu.HBM)
    anywhere = pl.BlockSpec(memory_space=pl.ANY)
    params = pltpu.CompilerParams(vmem_limit_bytes=24 * 2**20)
    plane = (SIDE, SIDE)
    f, mask = stay(populations.reshape(19, *plane)), stay(solid_mask.reshape(plane))
    message = in_vmem(8, SIDE)
    collided = (
        in_vmem(19, *plane), in_vmem(19, *plane), in_vmem(*plane), in_vmem(*plane),
        in_vmem(4, 8, SIDE),
    )
    work = [
        pltpu.VMEM(plane, jnp.int32), pltpu.VMEM(plane, F32),
        pltpu.SemaphoreType.DMA((CHUNKS + 1,)),
    ]
    pairs, codes = plan(n_bx, n_by)
    *x_msgs, picks, live_v, f_v, r_v, solid_v, active_v, y_pre = pl.pallas_call(
        rim_kernel,
        out_shape=(message,) * X_SLOTS + (in_vmem(4 + Y_SLOTS, 8, SIDE), in_vmem(4, 8, SIDE)) + collided,
        in_specs=[hbm] * 5,
        out_specs=[vmem] * (X_SLOTS + 7),
        scratch_shapes=[
            pltpu.VMEM((2, 19, 8, SIDE), F32), pltpu.VMEM((2, 8, SIDE), jnp.int32),
            pltpu.SMEM((1, n_bx), jnp.int32), pltpu.SMEM((1, 1, 4), jnp.int32),
            pltpu.SMEM(codes.shape, jnp.int32), *work, pltpu.SemaphoreType.DMA((7,)),
        ],
        compiler_params=params,
        name="rim",
    )(stay(pore_count.T), stay(pore_list), stay(jnp.asarray(codes)), f, mask)

    x_halos = [
        keep(lax.ppermute(message, ("bx", "by"), group)) for message, group in zip(x_msgs, pairs["x"])
    ]

    f_v, r_v, solid_v, active_v, y_pre = pl.pallas_call(
        collide_kernel,
        out_shape=collided,
        in_specs=[hbm] * 2 + [vmem] * 6,
        out_specs=[vmem] * 5,
        scratch_shapes=work,
        input_output_aliases={3: 0, 4: 1, 5: 2, 6: 3, 7: 4},
        compiler_params=params,
        cost_estimate=pl.CostEstimate(
            flops=8_000_000, bytes_accessed=4_000_000, transcendentals=0
        ),
        name="collide",
    )(f, mask, keep(live_v), *(keep(x) for x in (f_v, r_v, solid_v, active_v, y_pre)))

    y_msgs = pl.pallas_call(
        corner_kernel,
        out_shape=(message,) * Y_SLOTS,
        in_specs=[vmem] * (2 + X_SLOTS),
        out_specs=[vmem] * Y_SLOTS,
        compiler_params=params,
        name="corner",
    )(keep(y_pre), keep(picks), *x_halos)

    y_halos = [
        keep(lax.ppermute(message, ("bx", "by"), group)) for message, group in zip(y_msgs, pairs["y"])
    ]

    out, partial = pl.pallas_call(
        stream_kernel,
        out_shape=(shape(19, *plane), in_vmem(10, *plane)),
        in_specs=[vmem] * (5 + X_SLOTS),
        out_specs=[anywhere, vmem],
        scratch_shapes=[
            pltpu.VMEM((9, *plane), F32), pltpu.VMEM((2, 8, SIDE), F32),
            pltpu.SemaphoreType.DMA((PARTS * len(RUNS),)),
        ],
        compiler_params=params,
        cost_estimate=pl.CostEstimate(
            flops=8_000_000, bytes_accessed=4_000_000, transcendentals=0
        ),
        name="stream",
    )(keep(f_v), keep(r_v), keep(solid_v), keep(active_v), keep(picks), *x_halos)

    out = pl.pallas_call(
        patch_kernel,
        out_shape=shape(19, *plane),
        in_specs=[vmem] * 3 + [anywhere] + [vmem] * Y_SLOTS,
        out_specs=anywhere,
        scratch_shapes=[pltpu.VMEM((10, *plane), F32), pltpu.SemaphoreType.DMA((10,))],
        input_output_aliases={3: 0},
        compiler_params=params,
        name="patch",
    )(keep(y_pre), keep(picks), keep(partial), out, *y_halos)
    return out.reshape(19, 1, *plane)


def solution(mesh):
    placed = (P(None, None, "bx", "by"), P(None, "bx", "by"), P("bx", "by", None), P(None, "by"))
    return jax.shard_map(
        functools.partial(local, mesh.shape["bx"], mesh.shape["by"]),
        mesh=mesh,
        in_specs=placed,
        out_specs=P(None, None, "bx", "by"),
        check_vma=False,
    )
```

```python
import functools

import jax
import jax.numpy as jnp
import numpy as np
from jax import lax
from jax.experimental import pallas as pl
from jax.experimental.pallas import tpu as pltpu
from jax.sharding import PartitionSpec as P

F32 = jnp.float32
SIDE = 128
TILES = SIDE // 8
CHUNKS = 2
X_SLOTS, Y_SLOTS = 3, 3

PAIRS = (
    (1, 2, (1, 0, 0)),
    (3, 4, (0, 1, 0)),
    (5, 6, (0, 0, 1)),
    (7, 8, (1, 1, 0)),
    (9, 10, (1, -1, 0)),
    (11, 12, (1, 0, 1)),
    (13, 14, (1, 0, -1)),
    (15, 16, (0, 1, 1)),
    (17, 18, (0, 1, -1)),
)
VELOCITY = {0: (0, 0, 0)}
OPPOSITE = {0: 0}
for _k, _o, _c in PAIRS:
    VELOCITY[_k], VELOCITY[_o] = _c, tuple(-v for v in _c)
    OPPOSITE[_k], OPPOSITE[_o] = _o, _k
OMEGA_PLUS = 1.0 / 0.8
OMEGA_MINUS = 1.0 / (0.1875 / 0.3 + 0.5)

X_UP, X_DOWN = (1, 7, 9, 11, 13), (2, 8, 10, 12, 14)
Y_UP, Y_DOWN = (3, 7, 10, 15, 17), (4, 8, 9, 16, 18)
Y_ALL = Y_UP + Y_DOWN
REST = tuple(k for k in range(19) if k not in Y_ALL)
RUNS = ((0, 3), (5, 2), (11, 4))
PARTS = 4
FLAG_ROW = (5, 6, 7, 5, 5)


def iota(axis):
    return lax.broadcasted_iota(jnp.int32, (8, SIDE), axis)


def relax(f):
    total = {p: f[k] + f[o] for p, (k, o, _) in enumerate(PAIRS)}
    diff = {p: f[k] - f[o] for p, (k, o, _) in enumerate(PAIRS)}
    density = ((total[0] + total[1]) + (total[2] + total[3])) + (
        (total[4] + total[5]) + (total[6] + total[7])
    )
    density = density + (total[8] + f[0])
    jx = (diff[0] + diff[3]) + (diff[4] + diff[5]) + diff[6]
    jy = (diff[1] + diff[3]) + (diff[7] - diff[4]) + diff[8]
    jz = (diff[2] + diff[5]) + (diff[7] - diff[6]) - diff[8]
    inverse = 1.0 / density
    speed = (jx * inverse, jy * inverse, jz * inverse)
    square = speed[0] * speed[0] + speed[1] * speed[1] + speed[2] * speed[2]
    base = 1.0 - 1.5 * square
    out = {0: f[0] - OMEGA_PLUS * (f[0] - (density * base) * (1.0 / 3.0))}
    for p, (k, o, c) in enumerate(PAIRS):
        weight = 1.0 / 18.0 if p < 3 else 1.0 / 36.0
        dotted = None
        for axis in range(3):
            if c[axis]:
                term = speed[axis] if c[axis] > 0 else -speed[axis]
                dotted = term if dotted is None else dotted + term
        scaled = density * weight
        even = 0.5 * total[p] - scaled * (base + 4.5 * (dotted * dotted))
        odd = 0.5 * diff[p] - scaled * (3.0 * dotted)
        out[k] = f[k] - OMEGA_PLUS * even - OMEGA_MINUS * odd
        out[o] = f[o] - OMEGA_PLUS * even + OMEGA_MINUS * odd
    return out


def is_early():
    position = lax.axis_index("bx") + lax.axis_index("by")
    return jnp.logical_and(
        jnp.logical_and(
            lax.axis_index("bx") < lax.axis_size("bx") // 2,
            lax.axis_index("by") < lax.axis_size("by") // 2,
        ),
        position > 0,
    )


def live_blocks(count_ref, list_ref):
    count = count_ref[0, lax.axis_index("bx")]
    live = []
    for b in range(4):
        hit = jnp.int32(0)
        for s in range(4):
            found = jnp.logical_and(s < count, list_ref[0, 0, s] == b)
            hit = jnp.where(found, jnp.int32(1), hit)
        live.append(hit)
    return live


def collide_block(live_v, f_v, mask_v, r_v, solid_v, active_v, y_pre, columns):
    lane, row = iota(1), iota(0)
    rows = SIDE // CHUNKS

    def tile(t, carry):
        at = pl.ds(pl.multiple_of(t * 8, 8), 8)
        is_live = live_v[t // (TILES // 2)] != 0.0
        f = [f_v[k, at, :] for k in range(19)]
        out = relax(f)
        out = [jnp.where(is_live, out[k], f[k]) for k in range(19)]
        for k in range(19):
            r_v[k, at, :] = out[k]
        solid = mask_v[at, :].astype(F32)
        solid_v[at, :] = solid
        active_v[at, :] = jnp.where(jnp.logical_and(is_live, solid == 0.0), 1.0, 0.0)
        packed = jnp.zeros((8, SIDE), F32)
        for start, edge, pops in ((0, SIDE - 1, Y_UP), (8, 0, Y_DOWN)):
            for n, k in enumerate(pops):
                packed = jnp.where(lane == start + n, out[k][:, edge : edge + 1], packed)
            flags = jnp.logical_and(lane >= start + 5, lane < start + 8)
            packed = jnp.where(flags, solid[:, edge : edge + 1], packed)
        columns[at, :] = packed
        return carry

    for c in range(CHUNKS):
        lax.fori_loop(c * (rows // 8), (c + 1) * (rows // 8), tile, 0, unroll=rows // 8)

    turned = jnp.transpose(columns[...])
    high, low = turned[0:8, :], turned[8:16, :]
    fore = jnp.logical_or(row == 1, row == 6)
    back = jnp.logical_or(row == 2, row == 7)
    y_pre[0] = jnp.where(
        fore, pltpu.roll(high, 1, 1), jnp.where(back, pltpu.roll(high, SIDE - 1, 1), high)
    )
    y_pre[1] = jnp.where(
        fore, pltpu.roll(low, SIDE - 1, 1), jnp.where(back, pltpu.roll(low, 1, 1), low)
    )
    for slab, flags in ((2, low), (3, high)):
        free = jnp.broadcast_to(flags[5:6, :], (8, SIDE)) == 0.0
        y_pre[slab] = jnp.where(free, live_v[slab], 0.0)


def rim_kernel(
    count_hbm, list_hbm, plan_hbm, f_hbm, m_hbm, *refs,
):
    x_msgs, refs = refs[:X_SLOTS], refs[X_SLOTS:]
    (
        picks, live_v, r_v, solid_v, active_v, y_pre,
        edge_f, edge_m, count_ref, list_ref, plan_ref, f_v, mask_v, columns, sems,
    ) = refs
    ends = (pl.ds(SIDE - 8, 8), pl.ds(0, 8))
    pairs = [(count_hbm, count_ref), (list_hbm, list_ref), (plan_hbm, plan_ref)]
    for n, end in enumerate(ends):
        pairs += [(m_hbm.at[end, :], edge_m.at[n]), (f_hbm.at[:, end, :], edge_f.at[n])]
    copies = [pltpu.make_async_copy(s, t, sems.at[n]) for n, (s, t) in enumerate(pairs)]
    for copy in copies:
        copy.start()
    for copy in copies:
        copy.wait()
    live = live_blocks(count_ref, list_ref)
    lane = iota(1)
    for n, (left, right) in enumerate(((0, 1), (2, 3), (0, 2), (1, 3))):
        live_v[n] = jnp.where(lane < SIDE // 2, live[left], live[right]).astype(F32)
    messages = []
    for n, (pops, inner) in enumerate(((X_UP, 7), (X_DOWN, 0))):
        f = [edge_f[n, k] for k in range(19)]
        out = relax(f)
        is_live = live_v[1 - n] != 0.0
        solid = edge_m[n].astype(F32)
        rows = [jnp.where(is_live, out[k], f[k])[inner : inner + 1, :] for k in pops]
        rows += [solid[inner : inner + 1, :]] * 3
        messages.append(jnp.concatenate(rows, axis=0))
    up, down = messages
    code = plan_ref[0, lax.axis_index("bx") * lax.axis_size("by") + lax.axis_index("by")]
    for n in range(4):
        picks[n] = jnp.broadcast_to(lax.rem(code >> (2 * n), 4), (8, SIDE)).astype(F32)
    for n in range(X_SLOTS):
        x_msgs[n][...] = jnp.where(lax.rem(code >> (8 + n), 2) == 1, up, down)
    for n in range(Y_SLOTS):
        bit = lax.rem(code >> (8 + X_SLOTS + n), 2)
        picks[4 + n] = jnp.broadcast_to(bit, (8, SIDE)).astype(F32)

    @pl.when(is_early())
    def _():
        whole = [
            pltpu.make_async_copy(m_hbm, mask_v, sems.at[0]),
            pltpu.make_async_copy(f_hbm, f_v, sems.at[1]),
        ]
        for copy in whole:
            copy.start()
        for copy in whole:
            copy.wait()
        collide_block(live_v, f_v, mask_v, r_v, solid_v, active_v, y_pre, columns)


def collide_kernel(
    f_v, mask_v, live_v, r_in, solid_in, active_in, y_in,
    r_v, solid_v, active_v, y_pre, columns,
):
    del r_in, solid_in, active_in, y_in

    @pl.when(jnp.logical_not(is_early()))
    def _():
        collide_block(live_v, f_v, mask_v, r_v, solid_v, active_v, y_pre, columns)


def chosen(pick, refs):
    taken = refs[0][...]
    for n, ref in enumerate(refs[1:], 1):
        taken = jnp.where(pick == float(n), ref[...], taken)
    return taken


def corner_kernel(y_pre, picks, *refs):
    halos, y_msgs = refs[:X_SLOTS], refs[X_SLOTS:]
    low, high = chosen(picks[0], halos), chosen(picks[1], halos)
    lane, row = iota(1), iota(0)
    fore = jnp.logical_or(row == 1, row == 6)
    back = jnp.logical_or(row == 2, row == 7)
    first, last = lane == 0, lane == SIDE - 1
    up = jnp.where(jnp.logical_and(fore, first), pltpu.roll(low, 1, 1), y_pre[0])
    up = jnp.where(jnp.logical_and(back, last), high, up)
    down = jnp.where(jnp.logical_and(fore, last), pltpu.roll(high, SIDE - 1, 1), y_pre[1])
    down = jnp.where(jnp.logical_and(back, first), low, down)
    for n, message in enumerate(y_msgs):
        message[...] = jnp.where(picks[4 + n] == 1.0, up, down)


def stream_kernel(
    f_v, r_v, solid_v, active_v, picks, *refs,
):
    halos, (out_hbm, partial, stage, edges, sems) = refs[:X_SLOTS], refs[X_SLOTS:]
    edges[0], edges[1] = chosen(picks[0], halos), chosen(picks[1], halos)
    lane, row = iota(1), iota(0)
    top, bottom = row == 0, row == 7
    first, last = lane == 0, lane == SIDE - 1

    def tile(t, carry):
        at = pl.ds(pl.multiple_of(t * 8, 8), 8)
        before = pl.ds(jnp.maximum(t * 8 - 1, 0), 1)
        after = pl.ds(jnp.minimum(t * 8 + 8, SIDE - 1), 1)

        def shift_x(block, row_before, row_after, step, halo_row):
            if step == 0:
                return block
            if step > 0:
                edge = jnp.where(t == 0, edges[0, halo_row : halo_row + 1, :], row_before())
                return jnp.where(top, edge, pltpu.roll(block, 1, 0))
            edge = jnp.where(t == TILES - 1, edges[1, halo_row : halo_row + 1, :], row_after())
            return jnp.where(bottom, edge, pltpu.roll(block, 7, 0))

        def shift_y(block, step):
            if step == 0:
                return block
            return pltpu.roll(block, 1 if step > 0 else SIDE - 1, 1)

        solid = solid_v[at, :]
        active = active_v[at, :] != 0.0
        blocked = {}
        for sx in (-1, 0, 1):
            moved = shift_x(
                solid, lambda: solid_v[before, :], lambda: solid_v[after, :], sx, 5
            )
            for sy in (-1, 0, 1):
                if sx or sy:
                    hit = shift_y(moved, sy) != 0.0
                    if sy:
                        hit = jnp.logical_or(hit, first if sy > 0 else last)
                    blocked[sx, sy] = hit
        own = [r_v[k, at, :] for k in range(19)]
        for k in range(19):
            sx, sy, _ = VELOCITY[k]
            moved = own[k]
            if sx:
                halo_row = X_UP.index(k) if sx > 0 else X_DOWN.index(k)
                moved = shift_x(
                    moved, lambda: r_v[k, before, :], lambda: r_v[k, after, :], sx, halo_row
                )
            moved = shift_y(moved, sy)
            if sx or sy:
                moved = jnp.where(blocked[sx, sy], own[OPPOSITE[k]], moved)
            result = jnp.where(active, moved, f_v[k, at, :])
            if k in Y_ALL:
                partial[Y_ALL.index(k), at, :] = result
            else:
                stage[REST.index(k), at, :] = result
        return carry

    copies = []
    for part in range(PARTS):
        tiles = TILES // PARTS
        lax.fori_loop(part * tiles, (part + 1) * tiles, tile, 0, unroll=tiles)
        rows = pl.ds(part * tiles * 8, tiles * 8)
        for n, (start, count) in enumerate(RUNS):
            first = REST.index(start)
            copy = pltpu.make_async_copy(
                stage.at[first : first + count, rows, :],
                out_hbm.at[start : start + count, rows, :],
                sems.at[part * len(RUNS) + n],
            )
            copy.start()
            copies.append(copy)
    for copy in copies:
        copy.wait()


def patch_kernel(y_pre, picks, partial, started, *refs):
    del started
    halos, (out_hbm, stage, sems) = refs[:Y_SLOTS], refs[Y_SLOTS:]
    below, above = chosen(picks[2], halos), chosen(picks[3], halos)
    rows = []
    for message, slab in ((below, 2), (above, 3)):
        for n, flag in enumerate(FLAG_ROW):
            free = jnp.logical_and(message[flag : flag + 1, :] == 0.0, y_pre[slab, 0:1, :] != 0.0)
            rows.append(jnp.where(free, message[n : n + 1, :], jnp.nan))
    rows.append(jnp.zeros((6, SIDE), F32))
    turned = jnp.transpose(jnp.concatenate(rows, axis=0))
    lane = iota(1)
    copies = []
    for n, k in enumerate(Y_ALL):
        edge = lane == (0 if n < 5 else SIDE - 1)
        for t in range(TILES):
            at = pl.ds(8 * t, 8)
            value = jnp.broadcast_to(turned[8 * t : 8 * t + 8, n : n + 1], (8, SIDE))
            value = jnp.where(edge, value, jnp.nan)
            stage[n, at, :] = jnp.where(value == value, value, partial[n, at, :])
        copies.append(pltpu.make_async_copy(stage.at[n], out_hbm.at[k], sems.at[n]))
        copies[-1].start()
    for copy in copies:
        copy.wait()


def shape(*dims):
    return jax.ShapeDtypeStruct(dims, F32)


def in_vmem(*dims):
    return pltpu.VMEM(dims, F32)


def keep(x):
    return pltpu.with_memory_space_constraint(x, pltpu.VMEM)


def stay(x):
    return pltpu.with_memory_space_constraint(x, pltpu.HBM)


def slots(n_bx, n_by):
    chosen_slots = {}
    for x in range(n_bx):
        for y in range(n_by):
            if x % 2 == 0:
                slot = 1 if y == 0 else 2 if x == n_bx - 2 or (x == 0 and y == n_by // 2) else 0
            else:
                slot = 1 if y else 2 if x == n_bx - 1 else 0
            chosen_slots["x", x, y, 1] = chosen_slots["x", (x + 1) % n_bx, y, -1] = slot
            up, down = (x, y, 1), (x, (y + 1) % n_by, -1)
            for source, target in ((up, y + 1), (down, y)):
                ahead = x < n_bx // 2 and target in (0, n_by // 2 - 1)
                ahead = ahead or (1 < x < 2 * n_bx // 3 and y in (0, n_by // 2 - 2))
                chosen_slots["y", *source] = 1 if y % 2 else 0 if ahead else 2
            if x == 0 and (y < 4 or y >= n_by - 3):
                special = {0: 1, 1: 0, 2: 2, 3: 0, n_by - 3: 1, n_by - 2: 0, n_by - 1: 2}
                chosen_slots["y", *up] = chosen_slots["y", *down] = special[y]
    return chosen_slots


def plan(n_bx, n_by):
    chosen_slots = slots(n_bx, n_by)
    pairs = {"x": [[] for _ in range(X_SLOTS)], "y": [[] for _ in range(Y_SLOTS)]}
    codes = np.zeros((n_bx, n_by), np.int32)
    for (axis, x, y, step), slot in chosen_slots.items():
        to = ((x + step) % n_bx, y) if axis == "x" else (x, (y + step) % n_by)
        pairs[axis][slot].append((x * n_by + y, to[0] * n_by + to[1]))
        side = (0 if axis == "x" else 2) + (0 if step > 0 else 1)
        codes[to] += slot << (2 * side)
        if step > 0:
            codes[x, y] += 1 << (8 + slot + (0 if axis == "x" else X_SLOTS))
    for group in pairs["x"] + pairs["y"]:
        for end in zip(*group):
            assert len(set(end)) == len(end)
    return pairs, codes.reshape(1, -1)


def local(n_bx, n_by, populations, solid_mask, pore_list, pore_count):
    vmem = pl.BlockSpec(memory_space=pltpu.VMEM)
    hbm = pl.BlockSpec(memory_space=pltpu.HBM)
    anywhere = pl.BlockSpec(memory_space=pl.ANY)
    params = pltpu.CompilerParams(vmem_limit_bytes=24 * 2**20)
    plane = (SIDE, SIDE)
    f, mask = populations.reshape(19, *plane), solid_mask.reshape(plane)
    message = in_vmem(8, SIDE)
    collided = (
        in_vmem(19, *plane), in_vmem(*plane), in_vmem(*plane), in_vmem(4, 8, SIDE),
    )
    pairs, codes = plan(n_bx, n_by)
    *x_msgs, picks, live_v, r_v, solid_v, active_v, y_pre = pl.pallas_call(
        rim_kernel,
        out_shape=(message,) * X_SLOTS + (in_vmem(4 + Y_SLOTS, 8, SIDE), in_vmem(4, 8, SIDE)) + collided,
        in_specs=[hbm] * 5,
        out_specs=[vmem] * (X_SLOTS + 6),
        scratch_shapes=[
            pltpu.VMEM((2, 19, 8, SIDE), F32), pltpu.VMEM((2, 8, SIDE), jnp.int32),
            pltpu.SMEM((1, n_bx), jnp.int32), pltpu.SMEM((1, 1, 4), jnp.int32),
            pltpu.SMEM(codes.shape, jnp.int32), pltpu.VMEM((19, *plane), F32),
            pltpu.VMEM(plane, jnp.int32), pltpu.VMEM(plane, F32), pltpu.SemaphoreType.DMA((7,)),
        ],
        compiler_params=params,
        name="rim",
    )(stay(pore_count.T), stay(pore_list), stay(jnp.asarray(codes)), stay(f), stay(mask))

    x_halos = [
        keep(lax.ppermute(message, ("bx", "by"), group)) for message, group in zip(x_msgs, pairs["x"])
    ]

    f_v, mask_v, _ = lax.optimization_barrier((f, mask, live_v))

    r_v, solid_v, active_v, y_pre = pl.pallas_call(
        collide_kernel,
        out_shape=collided,
        in_specs=[vmem] * 7,
        out_specs=[vmem] * 4,
        scratch_shapes=[pltpu.VMEM(plane, F32)],
        input_output_aliases={3: 0, 4: 1, 5: 2, 6: 3},
        compiler_params=params,
        cost_estimate=pl.CostEstimate(
            flops=8_000_000, bytes_accessed=4_000_000, transcendentals=0
        ),
        name="collide",
    )(keep(f_v), keep(mask_v), keep(live_v), *(keep(x) for x in (r_v, solid_v, active_v, y_pre)))

    y_msgs = pl.pallas_call(
        corner_kernel,
        out_shape=(message,) * Y_SLOTS,
        in_specs=[vmem] * (2 + X_SLOTS),
        out_specs=[vmem] * Y_SLOTS,
        compiler_params=params,
        name="corner",
    )(keep(y_pre), keep(picks), *x_halos)

    y_halos = [
        keep(lax.ppermute(message, ("bx", "by"), group)) for message, group in zip(y_msgs, pairs["y"])
    ]

    out, partial = pl.pallas_call(
        stream_kernel,
        out_shape=(shape(19, *plane), in_vmem(10, *plane)),
        in_specs=[vmem] * (5 + X_SLOTS),
        out_specs=[anywhere, vmem],
        scratch_shapes=[
            pltpu.VMEM((9, *plane), F32), pltpu.VMEM((2, 8, SIDE), F32),
            pltpu.SemaphoreType.DMA((PARTS * len(RUNS),)),
        ],
        compiler_params=params,
        cost_estimate=pl.CostEstimate(
            flops=8_000_000, bytes_accessed=4_000_000, transcendentals=0
        ),
        name="stream",
    )(keep(f_v), keep(r_v), keep(solid_v), keep(active_v), keep(picks), *x_halos)

    out = pl.pallas_call(
        patch_kernel,
        out_shape=shape(19, *plane),
        in_specs=[vmem] * 3 + [anywhere] + [vmem] * Y_SLOTS,
        out_specs=anywhere,
        scratch_shapes=[pltpu.VMEM((10, *plane), F32), pltpu.SemaphoreType.DMA((10,))],
        input_output_aliases={3: 0},
        compiler_params=params,
        name="patch",
    )(keep(y_pre), keep(picks), keep(partial), out, *y_halos)
    return out.reshape(19, 1, *plane)


def solution(mesh):
    placed = (P(None, None, "bx", "by"), P(None, "bx", "by"), P("bx", "by", None), P(None, "by"))
    return jax.shard_map(
        functools.partial(local, mesh.shape["bx"], mesh.shape["by"]),
        mesh=mesh,
        in_specs=placed,
        out_specs=P(None, None, "bx", "by"),
        check_vma=False,
    )
```

```python
import functools

import jax
import jax.numpy as jnp
import numpy as np
from jax import lax
from jax.experimental import pallas as pl
from jax.experimental.pallas import tpu as pltpu
from jax.sharding import PartitionSpec as P

F32 = jnp.float32
SIDE = 128
TILES = SIDE // 8
CHUNKS = 2
X_SLOTS, Y_SLOTS = 3, 3

PAIRS = (
    (1, 2, (1, 0, 0)),
    (3, 4, (0, 1, 0)),
    (5, 6, (0, 0, 1)),
    (7, 8, (1, 1, 0)),
    (9, 10, (1, -1, 0)),
    (11, 12, (1, 0, 1)),
    (13, 14, (1, 0, -1)),
    (15, 16, (0, 1, 1)),
    (17, 18, (0, 1, -1)),
)
VELOCITY = {0: (0, 0, 0)}
OPPOSITE = {0: 0}
for _k, _o, _c in PAIRS:
    VELOCITY[_k], VELOCITY[_o] = _c, tuple(-v for v in _c)
    OPPOSITE[_k], OPPOSITE[_o] = _o, _k
OMEGA_PLUS = 1.0 / 0.8
OMEGA_MINUS = 1.0 / (0.1875 / 0.3 + 0.5)

X_UP, X_DOWN = (1, 7, 9, 11, 13), (2, 8, 10, 12, 14)
Y_UP, Y_DOWN = (3, 7, 10, 15, 17), (4, 8, 9, 16, 18)
Y_ALL = Y_UP + Y_DOWN
REST = tuple(k for k in range(19) if k not in Y_ALL)
RUNS = ((0, 3), (5, 2), (11, 4))
PARTS = 4
FLAG_ROW = (5, 6, 7, 5, 5)


def iota(axis):
    return lax.broadcasted_iota(jnp.int32, (8, SIDE), axis)


def relax(f):
    total = {p: f[k] + f[o] for p, (k, o, _) in enumerate(PAIRS)}
    diff = {p: f[k] - f[o] for p, (k, o, _) in enumerate(PAIRS)}
    density = ((total[0] + total[1]) + (total[2] + total[3])) + (
        (total[4] + total[5]) + (total[6] + total[7])
    )
    density = density + (total[8] + f[0])
    jx = (diff[0] + diff[3]) + (diff[4] + diff[5]) + diff[6]
    jy = (diff[1] + diff[3]) + (diff[7] - diff[4]) + diff[8]
    jz = (diff[2] + diff[5]) + (diff[7] - diff[6]) - diff[8]
    inverse = 1.0 / density
    speed = (jx * inverse, jy * inverse, jz * inverse)
    square = speed[0] * speed[0] + speed[1] * speed[1] + speed[2] * speed[2]
    base = 1.0 - 1.5 * square
    out = {0: f[0] - OMEGA_PLUS * (f[0] - (density * base) * (1.0 / 3.0))}
    for p, (k, o, c) in enumerate(PAIRS):
        weight = 1.0 / 18.0 if p < 3 else 1.0 / 36.0
        dotted = None
        for axis in range(3):
            if c[axis]:
                term = speed[axis] if c[axis] > 0 else -speed[axis]
                dotted = term if dotted is None else dotted + term
        scaled = density * weight
        even = 0.5 * total[p] - scaled * (base + 4.5 * (dotted * dotted))
        odd = 0.5 * diff[p] - scaled * (3.0 * dotted)
        out[k] = f[k] - OMEGA_PLUS * even - OMEGA_MINUS * odd
        out[o] = f[o] - OMEGA_PLUS * even + OMEGA_MINUS * odd
    return out


def is_early():
    position = lax.axis_index("bx") + lax.axis_index("by")
    return jnp.logical_and(
        jnp.logical_and(
            lax.axis_index("bx") < lax.axis_size("bx") // 2,
            lax.axis_index("by") < lax.axis_size("by") // 2,
        ),
        position > 0,
    )


def live_blocks(count_ref, list_ref):
    count = count_ref[0, lax.axis_index("bx")]
    live = []
    for b in range(4):
        hit = jnp.int32(0)
        for s in range(4):
            found = jnp.logical_and(s < count, list_ref[0, 0, s] == b)
            hit = jnp.where(found, jnp.int32(1), hit)
        live.append(hit)
    return live


def collide_block(live_v, f_v, mask_v, r_v, solid_v, active_v, y_pre, columns):
    lane, row = iota(1), iota(0)
    rows = SIDE // CHUNKS

    def tile(t, carry):
        at = pl.ds(pl.multiple_of(t * 8, 8), 8)
        is_live = live_v[t // (TILES // 2)] != 0.0
        f = [f_v[k, at, :] for k in range(19)]
        out = relax(f)
        out = [jnp.where(is_live, out[k], f[k]) for k in range(19)]
        for k in range(19):
            r_v[k, at, :] = out[k]
        solid = mask_v[at, :].astype(F32)
        solid_v[at, :] = solid
        active_v[at, :] = jnp.where(jnp.logical_and(is_live, solid == 0.0), 1.0, 0.0)
        packed = jnp.zeros((8, SIDE), F32)
        for start, edge, pops in ((0, SIDE - 1, Y_UP), (8, 0, Y_DOWN)):
            for n, k in enumerate(pops):
                packed = jnp.where(lane == start + n, out[k][:, edge : edge + 1], packed)
            flags = jnp.logical_and(lane >= start + 5, lane < start + 8)
            packed = jnp.where(flags, solid[:, edge : edge + 1], packed)
        columns[at, :] = packed
        return carry

    for c in range(CHUNKS):
        lax.fori_loop(c * (rows // 8), (c + 1) * (rows // 8), tile, 0, unroll=rows // 8)

    turned = jnp.transpose(columns[...])
    high, low = turned[0:8, :], turned[8:16, :]
    fore = jnp.logical_or(row == 1, row == 6)
    back = jnp.logical_or(row == 2, row == 7)
    y_pre[0] = jnp.where(
        fore, pltpu.roll(high, 1, 1), jnp.where(back, pltpu.roll(high, SIDE - 1, 1), high)
    )
    y_pre[1] = jnp.where(
        fore, pltpu.roll(low, SIDE - 1, 1), jnp.where(back, pltpu.roll(low, 1, 1), low)
    )
    for slab, flags in ((2, low), (3, high)):
        free = jnp.broadcast_to(flags[5:6, :], (8, SIDE)) == 0.0
        y_pre[slab] = jnp.where(free, live_v[slab], 0.0)


def rim_kernel(
    count_hbm, list_hbm, plan_hbm, f_hbm, m_hbm, *refs,
):
    x_msgs, refs = refs[:X_SLOTS], refs[X_SLOTS:]
    (
        picks, live_v, r_v, solid_v, active_v, y_pre,
        edge_f, edge_m, count_ref, list_ref, plan_ref, f_v, mask_v, columns, sems,
    ) = refs
    ends = (pl.ds(SIDE - 8, 8), pl.ds(0, 8))
    pairs = [(count_hbm, count_ref), (list_hbm, list_ref), (plan_hbm, plan_ref)]
    for n, end in enumerate(ends):
        pairs += [(m_hbm.at[end, :], edge_m.at[n]), (f_hbm.at[:, end, :], edge_f.at[n])]
    copies = [pltpu.make_async_copy(s, t, sems.at[n]) for n, (s, t) in enumerate(pairs)]
    for copy in copies:
        copy.start()
    for copy in copies:
        copy.wait()
    live = live_blocks(count_ref, list_ref)
    lane = iota(1)
    for n, (left, right) in enumerate(((0, 1), (2, 3), (0, 2), (1, 3))):
        live_v[n] = jnp.where(lane < SIDE // 2, live[left], live[right]).astype(F32)
    messages = []
    for n, (pops, inner) in enumerate(((X_UP, 7), (X_DOWN, 0))):
        f = [edge_f[n, k] for k in range(19)]
        out = relax(f)
        is_live = live_v[1 - n] != 0.0
        solid = edge_m[n].astype(F32)
        rows = [jnp.where(is_live, out[k], f[k])[inner : inner + 1, :] for k in pops]
        rows += [solid[inner : inner + 1, :]] * 3
        messages.append(jnp.concatenate(rows, axis=0))
    up, down = messages
    code = plan_ref[0, lax.axis_index("bx") * lax.axis_size("by") + lax.axis_index("by")]
    for n in range(4):
        picks[n] = jnp.broadcast_to(lax.rem(code >> (2 * n), 4), (8, SIDE)).astype(F32)
    for n in range(X_SLOTS):
        x_msgs[n][...] = jnp.where(lax.rem(code >> (8 + n), 2) == 1, up, down)
    for n in range(Y_SLOTS):
        bit = lax.rem(code >> (8 + X_SLOTS + n), 2)
        picks[4 + n] = jnp.broadcast_to(bit, (8, SIDE)).astype(F32)

    @pl.when(is_early())
    def _():
        whole = [
            pltpu.make_async_copy(m_hbm, mask_v, sems.at[0]),
            pltpu.make_async_copy(f_hbm, f_v, sems.at[1]),
        ]
        for copy in whole:
            copy.start()
        for copy in whole:
            copy.wait()
        collide_block(live_v, f_v, mask_v, r_v, solid_v, active_v, y_pre, columns)


def collide_kernel(
    f_v, mask_v, live_v, r_in, solid_in, active_in, y_in,
    r_v, solid_v, active_v, y_pre, columns,
):
    del r_in, solid_in, active_in, y_in

    @pl.when(jnp.logical_not(is_early()))
    def _():
        collide_block(live_v, f_v, mask_v, r_v, solid_v, active_v, y_pre, columns)


def chosen(pick, refs):
    taken = refs[0][...]
    for n, ref in enumerate(refs[1:], 1):
        taken = jnp.where(pick == float(n), ref[...], taken)
    return taken


def corner_kernel(y_pre, picks, *refs):
    halos, y_msgs = refs[:X_SLOTS], refs[X_SLOTS:]
    low, high = chosen(picks[0], halos), chosen(picks[1], halos)
    lane, row = iota(1), iota(0)
    fore = jnp.logical_or(row == 1, row == 6)
    back = jnp.logical_or(row == 2, row == 7)
    first, last = lane == 0, lane == SIDE - 1
    up = jnp.where(jnp.logical_and(fore, first), pltpu.roll(low, 1, 1), y_pre[0])
    up = jnp.where(jnp.logical_and(back, last), high, up)
    down = jnp.where(jnp.logical_and(fore, last), pltpu.roll(high, SIDE - 1, 1), y_pre[1])
    down = jnp.where(jnp.logical_and(back, first), low, down)
    for n, message in enumerate(y_msgs):
        message[...] = jnp.where(picks[4 + n] == 1.0, up, down)


def stream_kernel(
    f_v, r_v, solid_v, active_v, picks, *refs,
):
    halos, (out_hbm, partial, stage, edges, sems) = refs[:X_SLOTS], refs[X_SLOTS:]
    edges[0], edges[1] = chosen(picks[0], halos), chosen(picks[1], halos)
    lane, row = iota(1), iota(0)
    top, bottom = row == 0, row == 7
    first, last = lane == 0, lane == SIDE - 1

    def tile(t, carry):
        at = pl.ds(pl.multiple_of(t * 8, 8), 8)
        before = pl.ds(jnp.maximum(t * 8 - 1, 0), 1)
        after = pl.ds(jnp.minimum(t * 8 + 8, SIDE - 1), 1)

        def shift_x(block, row_before, row_after, step, halo_row):
            if step == 0:
                return block
            if step > 0:
                edge = jnp.where(t == 0, edges[0, halo_row : halo_row + 1, :], row_before())
                return jnp.where(top, edge, pltpu.roll(block, 1, 0))
            edge = jnp.where(t == TILES - 1, edges[1, halo_row : halo_row + 1, :], row_after())
            return jnp.where(bottom, edge, pltpu.roll(block, 7, 0))

        def shift_y(block, step):
            if step == 0:
                return block
            return pltpu.roll(block, 1 if step > 0 else SIDE - 1, 1)

        solid = solid_v[at, :]
        active = active_v[at, :] != 0.0
        blocked = {}
        for sx in (-1, 0, 1):
            moved = shift_x(
                solid, lambda: solid_v[before, :], lambda: solid_v[after, :], sx, 5
            )
            for sy in (-1, 0, 1):
                if sx or sy:
                    hit = shift_y(moved, sy) != 0.0
                    if sy:
                        hit = jnp.logical_or(hit, first if sy > 0 else last)
                    blocked[sx, sy] = hit
        own = [r_v[k, at, :] for k in range(19)]
        for k in range(19):
            sx, sy, _ = VELOCITY[k]
            moved = own[k]
            if sx:
                halo_row = X_UP.index(k) if sx > 0 else X_DOWN.index(k)
                moved = shift_x(
                    moved, lambda: r_v[k, before, :], lambda: r_v[k, after, :], sx, halo_row
                )
            moved = shift_y(moved, sy)
            if sx or sy:
                moved = jnp.where(blocked[sx, sy], own[OPPOSITE[k]], moved)
            result = jnp.where(active, moved, f_v[k, at, :])
            if k in Y_ALL:
                partial[Y_ALL.index(k), at, :] = result
            else:
                stage[REST.index(k), at, :] = result
        return carry

    copies = []
    for part in range(PARTS):
        tiles = TILES // PARTS
        lax.fori_loop(part * tiles, (part + 1) * tiles, tile, 0, unroll=tiles)
        rows = pl.ds(part * tiles * 8, tiles * 8)
        for n, (start, count) in enumerate(RUNS):
            first = REST.index(start)
            copy = pltpu.make_async_copy(
                stage.at[first : first + count, rows, :],
                out_hbm.at[start : start + count, rows, :],
                sems.at[part * len(RUNS) + n],
            )
            copy.start()
            copies.append(copy)
    for copy in copies:
        copy.wait()


def patch_kernel(y_pre, picks, partial, started, *refs):
    del started
    halos, (out_hbm, stage, sems) = refs[:Y_SLOTS], refs[Y_SLOTS:]
    below, above = chosen(picks[2], halos), chosen(picks[3], halos)
    rows = []
    for message, slab in ((below, 2), (above, 3)):
        for n, flag in enumerate(FLAG_ROW):
            free = jnp.logical_and(message[flag : flag + 1, :] == 0.0, y_pre[slab, 0:1, :] != 0.0)
            rows.append(jnp.where(free, message[n : n + 1, :], jnp.nan))
    rows.append(jnp.zeros((6, SIDE), F32))
    turned = jnp.transpose(jnp.concatenate(rows, axis=0))
    lane = iota(1)
    copies = []
    for n, k in enumerate(Y_ALL):
        edge = lane == (0 if n < 5 else SIDE - 1)
        for t in range(TILES):
            at = pl.ds(8 * t, 8)
            value = jnp.broadcast_to(turned[8 * t : 8 * t + 8, n : n + 1], (8, SIDE))
            value = jnp.where(edge, value, jnp.nan)
            stage[n, at, :] = jnp.where(value == value, value, partial[n, at, :])
        copies.append(pltpu.make_async_copy(stage.at[n], out_hbm.at[k], sems.at[n]))
        copies[-1].start()
    for copy in copies:
        copy.wait()


def shape(*dims):
    return jax.ShapeDtypeStruct(dims, F32)


def in_vmem(*dims):
    return pltpu.VMEM(dims, F32)


def keep(x):
    return pltpu.with_memory_space_constraint(x, pltpu.VMEM)


def stay(x):
    return pltpu.with_memory_space_constraint(x, pltpu.HBM)


def slots(n_bx, n_by):
    chosen_slots = {}
    half = n_by // 2
    for x in range(n_bx):
        for y in range(n_by):
            middle = 1 < y < half - 2
            if x % 2 == 0:
                slot = 1 if y == 0 or (x == n_bx - 2 and middle) else 2 if x == n_bx - 2 else 0
                slot = 2 if x == 0 and y == half else slot
            else:
                slot = 1 if y else 2 if x == n_bx - 1 else 0
                slot = 2 if x in (n_bx - 3, n_bx - 1) and middle else slot
            chosen_slots["x", x, y, 1] = chosen_slots["x", (x + 1) % n_bx, y, -1] = slot
            up, down = (x, y, 1), (x, (y + 1) % n_by, -1)
            for source, target in ((up, y + 1), (down, y)):
                ahead = x < n_bx // 2 and target in (0, half - 1)
                ahead = ahead or (1 < x < 2 * n_bx // 3 and y in (0, half - 2))
                ahead = ahead or (x == 1 and y == half - 2)
                ahead = ahead or (x == 0 and y in (0, 2, n_by - 2))
                chosen_slots["y", *source] = 1 if y % 2 else 0 if ahead else 2
    return chosen_slots


def plan(n_bx, n_by):
    chosen_slots = slots(n_bx, n_by)
    pairs = {"x": [[] for _ in range(X_SLOTS)], "y": [[] for _ in range(Y_SLOTS)]}
    codes = np.zeros((n_bx, n_by), np.int32)
    for (axis, x, y, step), slot in chosen_slots.items():
        to = ((x + step) % n_bx, y) if axis == "x" else (x, (y + step) % n_by)
        pairs[axis][slot].append((x * n_by + y, to[0] * n_by + to[1]))
        side = (0 if axis == "x" else 2) + (0 if step > 0 else 1)
        codes[to] += slot << (2 * side)
        if step > 0:
            codes[x, y] += 1 << (8 + slot + (0 if axis == "x" else X_SLOTS))
    for group in pairs["x"] + pairs["y"]:
        for end in zip(*group):
            assert len(set(end)) == len(end)
    return pairs, codes.reshape(1, -1)


def local(n_bx, n_by, populations, solid_mask, pore_list, pore_count):
    vmem = pl.BlockSpec(memory_space=pltpu.VMEM)
    hbm = pl.BlockSpec(memory_space=pltpu.HBM)
    anywhere = pl.BlockSpec(memory_space=pl.ANY)
    params = pltpu.CompilerParams(vmem_limit_bytes=24 * 2**20)
    plane = (SIDE, SIDE)
    f, mask = populations.reshape(19, *plane), solid_mask.reshape(plane)
    message = in_vmem(8, SIDE)
    collided = (
        in_vmem(19, *plane), in_vmem(*plane), in_vmem(*plane), in_vmem(4, 8, SIDE),
    )
    pairs, codes = plan(n_bx, n_by)
    *x_msgs, picks, live_v, r_v, solid_v, active_v, y_pre = pl.pallas_call(
        rim_kernel,
        out_shape=(message,) * X_SLOTS + (in_vmem(4 + Y_SLOTS, 8, SIDE), in_vmem(4, 8, SIDE)) + collided,
        in_specs=[hbm] * 5,
        out_specs=[vmem] * (X_SLOTS + 6),
        scratch_shapes=[
            pltpu.VMEM((2, 19, 8, SIDE), F32), pltpu.VMEM((2, 8, SIDE), jnp.int32),
            pltpu.SMEM((1, n_bx), jnp.int32), pltpu.SMEM((1, 1, 4), jnp.int32),
            pltpu.SMEM(codes.shape, jnp.int32), pltpu.VMEM((19, *plane), F32),
            pltpu.VMEM(plane, jnp.int32), pltpu.VMEM(plane, F32), pltpu.SemaphoreType.DMA((7,)),
        ],
        compiler_params=params,
        name="rim",
    )(stay(pore_count.T), stay(pore_list), stay(jnp.asarray(codes)), stay(f), stay(mask))

    x_halos = [
        keep(lax.ppermute(message, ("bx", "by"), group)) for message, group in zip(x_msgs, pairs["x"])
    ]

    f_v, mask_v, _ = lax.optimization_barrier((f, mask, live_v))

    r_v, solid_v, active_v, y_pre = pl.pallas_call(
        collide_kernel,
        out_shape=collided,
        in_specs=[vmem] * 7,
        out_specs=[vmem] * 4,
        scratch_shapes=[pltpu.VMEM(plane, F32)],
        input_output_aliases={3: 0, 4: 1, 5: 2, 6: 3},
        compiler_params=params,
        cost_estimate=pl.CostEstimate(
            flops=8_000_000, bytes_accessed=4_000_000, transcendentals=0
        ),
        name="collide",
    )(keep(f_v), keep(mask_v), keep(live_v), *(keep(x) for x in (r_v, solid_v, active_v, y_pre)))

    y_msgs = pl.pallas_call(
        corner_kernel,
        out_shape=(message,) * Y_SLOTS,
        in_specs=[vmem] * (2 + X_SLOTS),
        out_specs=[vmem] * Y_SLOTS,
        compiler_params=params,
        name="corner",
    )(keep(y_pre), keep(picks), *x_halos)

    y_halos = [
        keep(lax.ppermute(message, ("bx", "by"), group)) for message, group in zip(y_msgs, pairs["y"])
    ]

    out, partial = pl.pallas_call(
        stream_kernel,
        out_shape=(shape(19, *plane), in_vmem(10, *plane)),
        in_specs=[vmem] * (5 + X_SLOTS),
        out_specs=[anywhere, vmem],
        scratch_shapes=[
            pltpu.VMEM((9, *plane), F32), pltpu.VMEM((2, 8, SIDE), F32),
            pltpu.SemaphoreType.DMA((PARTS * len(RUNS),)),
        ],
        compiler_params=params,
        cost_estimate=pl.CostEstimate(
            flops=8_000_000, bytes_accessed=4_000_000, transcendentals=0
        ),
        name="stream",
    )(keep(f_v), keep(r_v), keep(solid_v), keep(active_v), keep(picks), *x_halos)

    out = pl.pallas_call(
        patch_kernel,
        out_shape=shape(19, *plane),
        in_specs=[vmem] * 3 + [anywhere] + [vmem] * Y_SLOTS,
        out_specs=anywhere,
        scratch_shapes=[pltpu.VMEM((10, *plane), F32), pltpu.SemaphoreType.DMA((10,))],
        input_output_aliases={3: 0},
        compiler_params=params,
        name="patch",
    )(keep(y_pre), keep(picks), keep(partial), out, *y_halos)
    return out.reshape(19, 1, *plane)


def solution(mesh):
    placed = (P(None, None, "bx", "by"), P(None, "bx", "by"), P("bx", "by", None), P(None, "by"))
    return jax.shard_map(
        functools.partial(local, mesh.shape["bx"], mesh.shape["by"]),
        mesh=mesh,
        in_specs=placed,
        out_specs=P(None, None, "bx", "by"),
        check_vma=False,
    )
```

```python
import functools

import jax
import jax.numpy as jnp
import numpy as np
from jax import lax
from jax.experimental import pallas as pl
from jax.experimental.pallas import tpu as pltpu
from jax.sharding import PartitionSpec as P

F32 = jnp.float32
SIDE = 128
TILES = SIDE // 8
CHUNKS = 2
X_SLOTS, Y_SLOTS = 3, 3

PAIRS = (
    (1, 2, (1, 0, 0)),
    (3, 4, (0, 1, 0)),
    (5, 6, (0, 0, 1)),
    (7, 8, (1, 1, 0)),
    (9, 10, (1, -1, 0)),
    (11, 12, (1, 0, 1)),
    (13, 14, (1, 0, -1)),
    (15, 16, (0, 1, 1)),
    (17, 18, (0, 1, -1)),
)
VELOCITY = {0: (0, 0, 0)}
OPPOSITE = {0: 0}
for _k, _o, _c in PAIRS:
    VELOCITY[_k], VELOCITY[_o] = _c, tuple(-v for v in _c)
    OPPOSITE[_k], OPPOSITE[_o] = _o, _k
OMEGA_PLUS = 1.0 / 0.8
OMEGA_MINUS = 1.0 / (0.1875 / 0.3 + 0.5)

X_UP, X_DOWN = (1, 7, 9, 11, 13), (2, 8, 10, 12, 14)
Y_UP, Y_DOWN = (3, 7, 10, 15, 17), (4, 8, 9, 16, 18)
Y_ALL = Y_UP + Y_DOWN
REST = tuple(k for k in range(19) if k not in Y_ALL)
RUNS = ((0, 3), (5, 2), (11, 4))
PARTS = 4
FLAG_ROW = (5, 6, 7, 5, 5)


def iota(axis):
    return lax.broadcasted_iota(jnp.int32, (8, SIDE), axis)


def relax(f):
    total = {p: f[k] + f[o] for p, (k, o, _) in enumerate(PAIRS)}
    diff = {p: f[k] - f[o] for p, (k, o, _) in enumerate(PAIRS)}
    density = ((total[0] + total[1]) + (total[2] + total[3])) + (
        (total[4] + total[5]) + (total[6] + total[7])
    )
    density = density + (total[8] + f[0])
    jx = (diff[0] + diff[3]) + (diff[4] + diff[5]) + diff[6]
    jy = (diff[1] + diff[3]) + (diff[7] - diff[4]) + diff[8]
    jz = (diff[2] + diff[5]) + (diff[7] - diff[6]) - diff[8]
    inverse = 1.0 / density
    speed = (jx * inverse, jy * inverse, jz * inverse)
    square = speed[0] * speed[0] + speed[1] * speed[1] + speed[2] * speed[2]
    base = 1.0 - 1.5 * square
    out = {0: f[0] - OMEGA_PLUS * (f[0] - (density * base) * (1.0 / 3.0))}
    for p, (k, o, c) in enumerate(PAIRS):
        weight = 1.0 / 18.0 if p < 3 else 1.0 / 36.0
        dotted = None
        for axis in range(3):
            if c[axis]:
                term = speed[axis] if c[axis] > 0 else -speed[axis]
                dotted = term if dotted is None else dotted + term
        scaled = density * weight
        even = 0.5 * total[p] - scaled * (base + 4.5 * (dotted * dotted))
        odd = 0.5 * diff[p] - scaled * (3.0 * dotted)
        out[k] = f[k] - OMEGA_PLUS * even - OMEGA_MINUS * odd
        out[o] = f[o] - OMEGA_PLUS * even + OMEGA_MINUS * odd
    return out


def is_early():
    position = lax.axis_index("bx") + lax.axis_index("by")
    return jnp.logical_and(
        jnp.logical_and(
            lax.axis_index("bx") < lax.axis_size("bx") // 2,
            lax.axis_index("by") < lax.axis_size("by") // 2,
        ),
        position > 0,
    )


def live_blocks(count_ref, list_ref):
    count = count_ref[0, lax.axis_index("bx")]
    live = []
    for b in range(4):
        hit = jnp.int32(0)
        for s in range(4):
            found = jnp.logical_and(s < count, list_ref[0, 0, s] == b)
            hit = jnp.where(found, jnp.int32(1), hit)
        live.append(hit)
    return live


def collide_block(live_v, f_v, mask_v, r_v, solid_v, active_v, y_pre, columns):
    lane, row = iota(1), iota(0)
    rows = SIDE // CHUNKS

    def tile(t, carry):
        at = pl.ds(pl.multiple_of(t * 8, 8), 8)
        is_live = live_v[t // (TILES // 2)] != 0.0
        f = [f_v[k, at, :] for k in range(19)]
        out = relax(f)
        out = [jnp.where(is_live, out[k], f[k]) for k in range(19)]
        for k in range(19):
            r_v[k, at, :] = out[k]
        solid = mask_v[at, :].astype(F32)
        solid_v[at, :] = solid
        active_v[at, :] = jnp.where(jnp.logical_and(is_live, solid == 0.0), 1.0, 0.0)
        packed = jnp.zeros((8, SIDE), F32)
        for start, edge, pops in ((0, SIDE - 1, Y_UP), (8, 0, Y_DOWN)):
            for n, k in enumerate(pops):
                packed = jnp.where(lane == start + n, out[k][:, edge : edge + 1], packed)
            flags = jnp.logical_and(lane >= start + 5, lane < start + 8)
            packed = jnp.where(flags, solid[:, edge : edge + 1], packed)
        columns[at, :] = packed
        return carry

    for c in range(CHUNKS):
        lax.fori_loop(c * (rows // 8), (c + 1) * (rows // 8), tile, 0, unroll=rows // 8)

    turned = jnp.transpose(columns[...])
    high, low = turned[0:8, :], turned[8:16, :]
    fore = jnp.logical_or(row == 1, row == 6)
    back = jnp.logical_or(row == 2, row == 7)
    y_pre[0] = jnp.where(
        fore, pltpu.roll(high, 1, 1), jnp.where(back, pltpu.roll(high, SIDE - 1, 1), high)
    )
    y_pre[1] = jnp.where(
        fore, pltpu.roll(low, SIDE - 1, 1), jnp.where(back, pltpu.roll(low, 1, 1), low)
    )
    for slab, flags in ((2, low), (3, high)):
        free = jnp.broadcast_to(flags[5:6, :], (8, SIDE)) == 0.0
        y_pre[slab] = jnp.where(free, live_v[slab], 0.0)


def rim_kernel(
    count_hbm, list_hbm, plan_hbm, f_hbm, m_hbm, *refs,
):
    x_msgs, refs = refs[:X_SLOTS], refs[X_SLOTS:]
    (
        picks, live_v, r_v, solid_v, active_v, y_pre,
        edge_f, edge_m, count_ref, list_ref, plan_ref, f_v, mask_v, columns, sems,
    ) = refs
    ends = (pl.ds(SIDE - 8, 8), pl.ds(0, 8))
    pairs = []
    for n, end in enumerate(ends):
        pairs += [(m_hbm.at[end, :], edge_m.at[n]), (f_hbm.at[:, end, :], edge_f.at[n])]
    pairs += [(count_hbm, count_ref), (list_hbm, list_ref), (plan_hbm, plan_ref)]
    copies = [pltpu.make_async_copy(s, t, sems.at[n]) for n, (s, t) in enumerate(pairs)]
    for copy in copies:
        copy.start()
    for copy in copies:
        copy.wait()
    live = live_blocks(count_ref, list_ref)
    lane = iota(1)
    for n, (left, right) in enumerate(((0, 1), (2, 3), (0, 2), (1, 3))):
        live_v[n] = jnp.where(lane < SIDE // 2, live[left], live[right]).astype(F32)
    messages = []
    for n, (pops, inner) in enumerate(((X_UP, 7), (X_DOWN, 0))):
        f = [edge_f[n, k] for k in range(19)]
        out = relax(f)
        is_live = live_v[1 - n] != 0.0
        solid = edge_m[n].astype(F32)
        rows = [jnp.where(is_live, out[k], f[k])[inner : inner + 1, :] for k in pops]
        rows += [solid[inner : inner + 1, :]] * 3
        messages.append(jnp.concatenate(rows, axis=0))
    up, down = messages
    code = plan_ref[0, lax.axis_index("bx") * lax.axis_size("by") + lax.axis_index("by")]
    for n in range(4):
        picks[n] = jnp.broadcast_to(lax.rem(code >> (2 * n), 4), (8, SIDE)).astype(F32)
    for n in range(X_SLOTS):
        x_msgs[n][...] = jnp.where(lax.rem(code >> (8 + n), 2) == 1, up, down)
    for n in range(Y_SLOTS):
        bit = lax.rem(code >> (8 + X_SLOTS + n), 2)
        picks[4 + n] = jnp.broadcast_to(bit, (8, SIDE)).astype(F32)

    @pl.when(is_early())
    def _():
        whole = [
            pltpu.make_async_copy(m_hbm, mask_v, sems.at[0]),
            pltpu.make_async_copy(f_hbm, f_v, sems.at[1]),
        ]
        for copy in whole:
            copy.start()
        for copy in whole:
            copy.wait()
        collide_block(live_v, f_v, mask_v, r_v, solid_v, active_v, y_pre, columns)


def collide_kernel(
    f_v, mask_v, live_v, r_in, solid_in, active_in, y_in,
    r_v, solid_v, active_v, y_pre, columns,
):
    del r_in, solid_in, active_in, y_in

    @pl.when(jnp.logical_not(is_early()))
    def _():
        collide_block(live_v, f_v, mask_v, r_v, solid_v, active_v, y_pre, columns)


def chosen(pick, refs):
    taken = refs[0][...]
    for n, ref in enumerate(refs[1:], 1):
        taken = jnp.where(pick == float(n), ref[...], taken)
    return taken


def corner_kernel(y_pre, picks, *refs):
    halos, y_msgs = refs[:X_SLOTS], refs[X_SLOTS:]
    low, high = chosen(picks[0], halos), chosen(picks[1], halos)
    lane, row = iota(1), iota(0)
    fore = jnp.logical_or(row == 1, row == 6)
    back = jnp.logical_or(row == 2, row == 7)
    first, last = lane == 0, lane == SIDE - 1
    up = jnp.where(jnp.logical_and(fore, first), pltpu.roll(low, 1, 1), y_pre[0])
    up = jnp.where(jnp.logical_and(back, last), high, up)
    down = jnp.where(jnp.logical_and(fore, last), pltpu.roll(high, SIDE - 1, 1), y_pre[1])
    down = jnp.where(jnp.logical_and(back, first), low, down)
    for n, message in enumerate(y_msgs):
        message[...] = jnp.where(picks[4 + n] == 1.0, up, down)


def stream_kernel(
    f_v, r_v, solid_v, active_v, picks, *refs,
):
    halos, (out_hbm, partial, stage, edges, sems) = refs[:X_SLOTS], refs[X_SLOTS:]
    edges[0], edges[1] = chosen(picks[0], halos), chosen(picks[1], halos)
    lane, row = iota(1), iota(0)
    top, bottom = row == 0, row == 7
    first, last = lane == 0, lane == SIDE - 1

    def tile(t, carry):
        at = pl.ds(pl.multiple_of(t * 8, 8), 8)
        before = pl.ds(jnp.maximum(t * 8 - 1, 0), 1)
        after = pl.ds(jnp.minimum(t * 8 + 8, SIDE - 1), 1)

        def shift_x(block, row_before, row_after, step, halo_row):
            if step == 0:
                return block
            if step > 0:
                edge = jnp.where(t == 0, edges[0, halo_row : halo_row + 1, :], row_before())
                return jnp.where(top, edge, pltpu.roll(block, 1, 0))
            edge = jnp.where(t == TILES - 1, edges[1, halo_row : halo_row + 1, :], row_after())
            return jnp.where(bottom, edge, pltpu.roll(block, 7, 0))

        def shift_y(block, step):
            if step == 0:
                return block
            return pltpu.roll(block, 1 if step > 0 else SIDE - 1, 1)

        solid = solid_v[at, :]
        active = active_v[at, :] != 0.0
        blocked = {}
        for sx in (-1, 0, 1):
            moved = shift_x(
                solid, lambda: solid_v[before, :], lambda: solid_v[after, :], sx, 5
            )
            for sy in (-1, 0, 1):
                if sx or sy:
                    hit = shift_y(moved, sy) != 0.0
                    if sy:
                        hit = jnp.logical_or(hit, first if sy > 0 else last)
                    blocked[sx, sy] = hit
        own = [r_v[k, at, :] for k in range(19)]
        for k in range(19):
            sx, sy, _ = VELOCITY[k]
            moved = own[k]
            if sx:
                halo_row = X_UP.index(k) if sx > 0 else X_DOWN.index(k)
                moved = shift_x(
                    moved, lambda: r_v[k, before, :], lambda: r_v[k, after, :], sx, halo_row
                )
            moved = shift_y(moved, sy)
            if sx or sy:
                moved = jnp.where(blocked[sx, sy], own[OPPOSITE[k]], moved)
            result = jnp.where(active, moved, f_v[k, at, :])
            if k in Y_ALL:
                partial[Y_ALL.index(k), at, :] = result
            else:
                stage[REST.index(k), at, :] = result
        return carry

    copies = []
    for part in range(PARTS):
        tiles = TILES // PARTS
        lax.fori_loop(part * tiles, (part + 1) * tiles, tile, 0, unroll=tiles)
        rows = pl.ds(part * tiles * 8, tiles * 8)
        for n, (start, count) in enumerate(RUNS):
            first = REST.index(start)
            copy = pltpu.make_async_copy(
                stage.at[first : first + count, rows, :],
                out_hbm.at[start : start + count, rows, :],
                sems.at[part * len(RUNS) + n],
            )
            copy.start()
            copies.append(copy)
    for copy in copies:
        copy.wait()


def patch_kernel(y_pre, picks, partial, started, *refs):
    del started
    halos, (out_hbm, stage, sems) = refs[:Y_SLOTS], refs[Y_SLOTS:]
    below, above = chosen(picks[2], halos), chosen(picks[3], halos)
    rows = []
    for message, slab in ((below, 2), (above, 3)):
        for n, flag in enumerate(FLAG_ROW):
            free = jnp.logical_and(message[flag : flag + 1, :] == 0.0, y_pre[slab, 0:1, :] != 0.0)
            rows.append(jnp.where(free, message[n : n + 1, :], jnp.nan))
    rows.append(jnp.zeros((6, SIDE), F32))
    turned = jnp.transpose(jnp.concatenate(rows, axis=0))
    lane = iota(1)
    copies = []
    for n, k in enumerate(Y_ALL):
        edge = lane == (0 if n < 5 else SIDE - 1)
        for t in range(TILES):
            at = pl.ds(8 * t, 8)
            value = jnp.broadcast_to(turned[8 * t : 8 * t + 8, n : n + 1], (8, SIDE))
            value = jnp.where(edge, value, jnp.nan)
            stage[n, at, :] = jnp.where(value == value, value, partial[n, at, :])
        copies.append(pltpu.make_async_copy(stage.at[n], out_hbm.at[k], sems.at[n]))
        copies[-1].start()
    for copy in copies:
        copy.wait()


def shape(*dims):
    return jax.ShapeDtypeStruct(dims, F32)


def in_vmem(*dims):
    return pltpu.VMEM(dims, F32)


def keep(x):
    return pltpu.with_memory_space_constraint(x, pltpu.VMEM)


def stay(x):
    return pltpu.with_memory_space_constraint(x, pltpu.HBM)


def slots(n_bx, n_by):
    chosen_slots = {}
    half = n_by // 2
    for x in range(n_bx):
        for y in range(n_by):
            middle = 1 < y < half - 2
            if x % 2 == 0:
                slot = 1 if y == 0 or (x == n_bx - 2 and middle) else 2 if x == n_bx - 2 else 0
                slot = 2 if x == 0 and y == half else slot
            else:
                slot = 1 if y else 2 if x == n_bx - 1 else 0
                slot = 2 if x in (n_bx - 3, n_bx - 1) and middle else slot
            chosen_slots["x", x, y, 1] = chosen_slots["x", (x + 1) % n_bx, y, -1] = slot
            up, down = (x, y, 1), (x, (y + 1) % n_by, -1)
            for source, target in ((up, y + 1), (down, y)):
                ahead = x < n_bx // 2 and target in (0, half - 1)
                ahead = ahead or (1 < x < 2 * n_bx // 3 and y in (0, half - 2))
                ahead = ahead or (x == 1 and y == half - 2)
                ahead = ahead or (x == 0 and y in (0, 2, n_by - 2))
                chosen_slots["y", *source] = 1 if y % 2 else 0 if ahead else 2
    return chosen_slots


def plan(n_bx, n_by):
    chosen_slots = slots(n_bx, n_by)
    pairs = {"x": [[] for _ in range(X_SLOTS)], "y": [[] for _ in range(Y_SLOTS)]}
    codes = np.zeros((n_bx, n_by), np.int32)
    for (axis, x, y, step), slot in chosen_slots.items():
        to = ((x + step) % n_bx, y) if axis == "x" else (x, (y + step) % n_by)
        pairs[axis][slot].append((x * n_by + y, to[0] * n_by + to[1]))
        side = (0 if axis == "x" else 2) + (0 if step > 0 else 1)
        codes[to] += slot << (2 * side)
        if step > 0:
            codes[x, y] += 1 << (8 + slot + (0 if axis == "x" else X_SLOTS))
    for group in pairs["x"] + pairs["y"]:
        for end in zip(*group):
            assert len(set(end)) == len(end)
    return pairs, codes.reshape(1, -1)


def local(n_bx, n_by, populations, solid_mask, pore_list, pore_count):
    vmem = pl.BlockSpec(memory_space=pltpu.VMEM)
    hbm = pl.BlockSpec(memory_space=pltpu.HBM)
    anywhere = pl.BlockSpec(memory_space=pl.ANY)
    params = pltpu.CompilerParams(vmem_limit_bytes=24 * 2**20)
    plane = (SIDE, SIDE)
    f, mask = populations.reshape(19, *plane), solid_mask.reshape(plane)
    message = in_vmem(8, SIDE)
    collided = (
        in_vmem(19, *plane), in_vmem(*plane), in_vmem(*plane), in_vmem(4, 8, SIDE),
    )
    pairs, codes = plan(n_bx, n_by)
    *x_msgs, picks, live_v, r_v, solid_v, active_v, y_pre = pl.pallas_call(
        rim_kernel,
        out_shape=(message,) * X_SLOTS + (in_vmem(4 + Y_SLOTS, 8, SIDE), in_vmem(4, 8, SIDE)) + collided,
        in_specs=[hbm] * 5,
        out_specs=[vmem] * (X_SLOTS + 6),
        scratch_shapes=[
            pltpu.VMEM((2, 19, 8, SIDE), F32), pltpu.VMEM((2, 8, SIDE), jnp.int32),
            pltpu.SMEM((1, n_bx), jnp.int32), pltpu.SMEM((1, 1, 4), jnp.int32),
            pltpu.SMEM(codes.shape, jnp.int32), pltpu.VMEM((19, *plane), F32),
            pltpu.VMEM(plane, jnp.int32), pltpu.VMEM(plane, F32), pltpu.SemaphoreType.DMA((7,)),
        ],
        compiler_params=params,
        name="rim",
    )(stay(pore_count.T), stay(pore_list), stay(jnp.asarray(codes)), stay(f), stay(mask))

    x_halos = [
        keep(lax.ppermute(message, ("bx", "by"), group)) for message, group in zip(x_msgs, pairs["x"])
    ]

    f_v, mask_v, _ = lax.optimization_barrier((f, mask, live_v))

    r_v, solid_v, active_v, y_pre = pl.pallas_call(
        collide_kernel,
        out_shape=collided,
        in_specs=[vmem] * 7,
        out_specs=[vmem] * 4,
        scratch_shapes=[pltpu.VMEM(plane, F32)],
        input_output_aliases={3: 0, 4: 1, 5: 2, 6: 3},
        compiler_params=params,
        cost_estimate=pl.CostEstimate(
            flops=8_000_000, bytes_accessed=4_000_000, transcendentals=0
        ),
        name="collide",
    )(keep(f_v), keep(mask_v), keep(live_v), *(keep(x) for x in (r_v, solid_v, active_v, y_pre)))

    y_msgs = pl.pallas_call(
        corner_kernel,
        out_shape=(message,) * Y_SLOTS,
        in_specs=[vmem] * (2 + X_SLOTS),
        out_specs=[vmem] * Y_SLOTS,
        compiler_params=params,
        name="corner",
    )(keep(y_pre), keep(picks), *x_halos)

    y_halos = [
        keep(lax.ppermute(message, ("bx", "by"), group)) for message, group in zip(y_msgs, pairs["y"])
    ]

    out, partial = pl.pallas_call(
        stream_kernel,
        out_shape=(shape(19, *plane), in_vmem(10, *plane)),
        in_specs=[vmem] * (5 + X_SLOTS),
        out_specs=[anywhere, vmem],
        scratch_shapes=[
            pltpu.VMEM((9, *plane), F32), pltpu.VMEM((2, 8, SIDE), F32),
            pltpu.SemaphoreType.DMA((PARTS * len(RUNS),)),
        ],
        compiler_params=params,
        cost_estimate=pl.CostEstimate(
            flops=8_000_000, bytes_accessed=4_000_000, transcendentals=0
        ),
        name="stream",
    )(keep(f_v), keep(r_v), keep(solid_v), keep(active_v), keep(picks), *x_halos)

    out = pl.pallas_call(
        patch_kernel,
        out_shape=shape(19, *plane),
        in_specs=[vmem] * 3 + [anywhere] + [vmem] * Y_SLOTS,
        out_specs=anywhere,
        scratch_shapes=[pltpu.VMEM((10, *plane), F32), pltpu.SemaphoreType.DMA((10,))],
        input_output_aliases={3: 0},
        compiler_params=params,
        name="patch",
    )(keep(y_pre), keep(picks), keep(partial), out, *y_halos)
    return out.reshape(19, 1, *plane)


def solution(mesh):
    placed = (P(None, None, "bx", "by"), P(None, "bx", "by"), P("bx", "by", None), P(None, "by"))
    return jax.shard_map(
        functools.partial(local, mesh.shape["bx"], mesh.shape["by"]),
        mesh=mesh,
        in_specs=placed,
        out_specs=P(None, None, "bx", "by"),
        check_vma=False,
    )
```
